32 devices in a mesh: dp: 4 (over x, core), seq: 8 (over z, y).
Axes of the slice: x: 2, y: 2, z: 4, core: 2. Of those that a mesh axis runs over, the one named last changes fastest.
Arguments:
- tokens: bfloat16 [24, 3072, 512], P('dp', 'seq'), may hold values from -6 to 6
- short_counts: int32 [4], P('dp'), may hold values from 1 to 5, as said below
- norm1_gain: bfloat16 [512], replicated, may hold values from 0.5 to 1.5
- norm1_bias: bfloat16 [512], replicated, may hold values from -1.25 to 1.25
- query_weight: bfloat16 [512, 512], replicated, may hold values from -0.25 to 0.25
- query_bias: bfloat16 [512], replicated, may hold values from -1.25 to 1.25
- key_weight: bfloat16 [512, 512], replicated, may hold values from -0.25 to 0.25
- key_bias: bfloat16 [512], replicated, may hold values from -1.25 to 1.25
- value_weight: bfloat16 [512, 512], replicated, may hold values from -0.25 to 0.25
- value_bias: bfloat16 [512], replicated, may hold values from -1.25 to 1.25
- output_weight: bfloat16 [512, 512], replicated, may hold values from -1.5 to 1.5
- output_bias: bfloat16 [512], replicated, may hold values from -1.25 to 1.25
- norm2_gain: bfloat16 [512], replicated, may hold values from 0.5 to 1.5
- norm2_bias: bfloat16 [512], replicated, may hold values from -1.25 to 1.25
- hidden_weight: bfloat16 [512, 2048], replicated, may hold values from -0.25 to 0.25
- hidden_bias: bfloat16 [2048], replicated, may hold values from -1.25 to 1.25
- return_weight: bfloat16 [2048, 512], replicated, may hold values from -0.125 to 0.125
- return_bias: bfloat16 [512], replicated, may hold values from -1.25 to 1.25
- cotangent: bfloat16 [24, 3072, 512], P('dp', 'seq'), may hold values from -6 to 6
Outputs:
- layer_out: bfloat16 [24, 3072, 512], P('dp', 'seq')
- input_grad: bfloat16 [24, 3072, 512], P('dp', 'seq')
- den_peak: float32 [], replicated
- grad_norm1_gain: float32 [512], replicated
- grad_norm1_bias: float32 [512], replicated
- grad_query_weight: float32 [512, 512], replicated
- grad_query_bias: float32 [512], replicated
- grad_key_weight: float32 [512, 512], replicated
- grad_key_bias: float32 [512], replicated
- grad_value_weight: float32 [512, 512], replicated
- grad_value_bias: float32 [512], replicated
- grad_output_weight: float32 [512, 512], replicated
- grad_output_bias: float32 [512], replicated
- grad_norm2_gain: float32 [512], replicated
- grad_norm2_bias: float32 [512], replicated
- grad_hidden_weight: float32 [512, 2048], replicated
- grad_hidden_bias: float32 [2048], replicated
- grad_return_weight: float32 [2048, 512], replicated
- grad_return_bias: float32 [512], replicated
The draws below stay inside these ranges and needn't reach their ends.
Inputs may be any that keep to these rules, and one draw needn't show every extreme that they name: `short_counts`: each dp index has at least one image of each resolution; every draw has an index with a single short image and one with 5.
All inputs are finite; a program needn't handle non-finite values.
Results may differ from the reference program's by a relative error of at most 0.012.
Values sent between devices are 32-bit elements; how exact they have to be, the bound alone decides.
A program may use at most 320 MiB of HBM per device.

```python
import jax
import jax.numpy as jnp
from jax import lax

D = 512
HEADS = 8
FF = 2048
HEAD_DIM = 64
ROWS = 6
LEN_LONG = 3072
LEN_SHORT = 784
GROUP = 384
LENGTH = 3072
IMAGES = 24
N_DP = 4


def draw_short_counts(key, part):
    key = jax.random.fold_in(key, 7)
    first, second = jax.random.split(key)
    counts = jax.random.randint(first, (N_DP,), 1, ROWS, dtype=jnp.int32)
    order = jax.random.permutation(second, N_DP)
    counts = counts.at[order[0]].set(1)
    counts = counts.at[order[1]].set(ROWS - 1)
    return counts


def shard_levels(rng, dims, cuts, low, largest):
    def one(axis_at, blocks):
        draws = jax.random.uniform(jax.random.fold_in(jax.random.fold_in(rng, 6), axis_at), (blocks,), jnp.float32, low / len(cuts), largest / len(cuts))
        return jnp.repeat(jnp.exp(draws), dims[axis_at] // blocks).reshape((-1,) + (1,) * (len(dims) - axis_at - 1))

    loudness = one(*cuts[0])
    for cut in cuts[1:]:
        loudness = loudness * one(*cut)
    return loudness


def normal_values(key, dims, deviation, most, cuts=(), kind=jnp.bfloat16):
    drawn = deviation * jax.random.normal(key, dims, jnp.float32)
    if cuts:
        drawn = drawn * shard_levels(key, dims, cuts, -0.22, 0.18)
    return jnp.clip(drawn, -most, most).astype(kind)


def setup_inputs(seed: int = 0) -> dict:
    splits = jax.random.split(jax.random.key(seed), 20)
    return {
        "tokens": normal_values(splits[0], (IMAGES, LENGTH, D), 1.0, 6.0, ((0, 4), (1, 8))),
        "short_counts": draw_short_counts(jax.random.fold_in(splits[19], 71), 0),
        "norm1_gain": jnp.clip(1.0 + 0.1 * jax.random.normal(splits[2], (D,), jnp.float32), 0.5, 1.5).astype(jnp.bfloat16),
        "norm1_bias": normal_values(splits[3], (D,), 0.2, 1.25),
        "query_weight": normal_values(splits[4], (D, D), D ** -0.5, 0.25),
        "query_bias": normal_values(splits[5], (D,), 0.2, 1.25),
        "key_weight": normal_values(splits[6], (D, D), D ** -0.5, 0.25),
        "key_bias": normal_values(splits[7], (D,), 0.2, 1.25),
        "value_weight": normal_values(splits[8], (D, D), D ** -0.5, 0.25),
        "value_bias": normal_values(splits[9], (D,), 0.2, 1.25),
        "output_weight": normal_values(splits[10], (D, D), (D // 32) ** -0.5, 1.5),
        "output_bias": normal_values(splits[11], (D,), 0.2, 1.25),
        "norm2_gain": jnp.clip(1.0 + 0.1 * jax.random.normal(splits[12], (D,), jnp.float32), 0.5, 1.5).astype(jnp.bfloat16),
        "norm2_bias": normal_values(splits[13], (D,), 0.2, 1.25),
        "hidden_weight": normal_values(splits[14], (D, FF), D ** -0.5, 0.25),
        "hidden_bias": normal_values(splits[15], (FF,), 0.2, 1.25),
        "return_weight": normal_values(splits[16], (FF, D), FF ** -0.5, 0.125),
        "return_bias": normal_values(splits[17], (D,), 0.2, 1.25),
        "cotangent": normal_values(splits[18], (IMAGES, LENGTH, D), 1.0, 6.0, ((0, 4), (1, 8))),
    }


@jax.custom_vjp
def low(v):
    return lax.optimization_barrier(v.astype(jnp.bfloat16)).astype(jnp.float32)

@jax.custom_vjp
def low_back(v):
    return v

def low_keep(v):
    return (low(v), None)

def low_pass(kept, grad):
    return (grad,)

def back_keep(v):
    return (v, None)

def back_low(kept, grad):
    return (low(grad),)
low.defvjp(low_keep, low_pass)
low_back.defvjp(back_keep, back_low)
EPSILON = 1e-05
HIGH = lax.Precision.HIGHEST

def layer_norm(values, gain, shift):
    centre = values - lax.optimization_barrier(jnp.mean(values, axis=-1, keepdims=True))
    spread = lax.optimization_barrier(jnp.mean(centre * centre, axis=-1, keepdims=True))
    return centre * lax.rsqrt(spread + EPSILON) * gain + shift

def feature(values):
    return jnp.where(values > 0, values + 1.0, jnp.exp(jnp.minimum(values, 0.0)))

def attend(query_feat, key_feat, value_low):
    blocks = LENGTH // GROUP
    shape = (blocks, GROUP, HEADS, HEAD_DIM)
    lower = jnp.tril(jnp.ones((GROUP, GROUP), jnp.float32))

    def advance(carry, block):
        state, key_sum = carry
        query_block, key_block, value_block = block
        scores = jnp.einsum('thd,shd->hts', query_block, key_block, precision=HIGH) * lower
        numer = jnp.einsum('hts,she->the', scores, value_block, precision=HIGH)
        numer = numer + jnp.einsum('thd,hde->the', query_block, state, precision=HIGH)
        denom = lax.optimization_barrier(jnp.sum(scores, axis=2)).T + jnp.einsum('thd,hd->th', query_block, key_sum, precision=HIGH)
        state = state + jnp.einsum('shd,she->hde', key_block, value_block, precision=HIGH)
        key_sum = key_sum + lax.optimization_barrier(jnp.sum(key_block, axis=0))
        return ((state, key_sum), (numer / denom[:, :, None], denom))
    start = (jnp.zeros((HEADS, HEAD_DIM, HEAD_DIM), jnp.float32), jnp.zeros((HEADS, HEAD_DIM), jnp.float32))
    parts = (query_feat.reshape(shape), key_feat.reshape(shape), value_low.reshape(shape))
    unused, (mixed, denom) = lax.scan(jax.checkpoint(advance), start, parts)
    return (mixed.reshape(LENGTH, D), denom.reshape(LENGTH, HEADS))

def forward(params, stream, valid):
    gain_one, shift_one, query_weight, query_bias, key_weight, key_bias, value_weight, value_bias, output_weight, output_bias, gain_two, shift_two, hidden_weight, hidden_bias, return_weight, return_bias = params
    first_in = low(layer_norm(stream, gain_one, shift_one))
    query_pre = low_back(jnp.dot(first_in, query_weight, precision=HIGH) + query_bias)
    key_pre = low_back(jnp.dot(first_in, key_weight, precision=HIGH) + key_bias)
    value_low = low(low_back(jnp.dot(first_in, value_weight, precision=HIGH) + value_bias))
    query_feat = low(feature(query_pre))
    key_feat = low(feature(key_pre) * valid[:, None])
    mixed, denom = attend(query_feat.reshape(LENGTH, HEADS, HEAD_DIM), key_feat.reshape(LENGTH, HEADS, HEAD_DIM), value_low.reshape(LENGTH, HEADS, HEAD_DIM))
    attn = low(mixed)
    middle = stream + low_back(jnp.dot(attn, output_weight, precision=HIGH) + output_bias)
    second_in = low(layer_norm(middle, gain_two, shift_two))
    hidden_pre = low_back(jnp.dot(second_in, hidden_weight, precision=HIGH) + hidden_bias)
    act = low(jax.nn.gelu(hidden_pre, approximate=False))
    result = middle + low_back(jnp.dot(act, return_weight, precision=HIGH) + return_bias)
    return (result, denom)

def reference(tokens, short_counts, norm1_gain, norm1_bias, query_weight, query_bias, key_weight, key_bias, value_weight, value_bias, output_weight, output_bias, norm2_gain, norm2_bias, hidden_weight, hidden_bias, return_weight, return_bias, cotangent):
    params = tuple((item.astype(jnp.float32) for item in (norm1_gain, norm1_bias, query_weight, query_bias, key_weight, key_bias, value_weight, value_bias, output_weight, output_bias, norm2_gain, norm2_bias, hidden_weight, hidden_bias, return_weight, return_bias)))
    image_ids = jnp.arange(tokens.shape[0], dtype=jnp.int32)
    short = image_ids % ROWS < short_counts[image_ids // ROWS]
    limits = jnp.where(short, LEN_SHORT, LEN_LONG).astype(jnp.int32)
    positions = jnp.arange(LENGTH, dtype=jnp.int32)

    def per_image(totals, item):
        image, grad_in, limit = item
        valid = (positions < limit).astype(jnp.float32)

        def local(weights, values):
            return forward(weights, values, valid)
        result, pull, denom = jax.vjp(local, params, image.astype(jnp.float32), has_aux=True)
        weight_grads, stream_grad = pull(grad_in.astype(jnp.float32))
        totals = jax.tree.map(lambda first, second: first + second, totals, weight_grads)
        peak = jnp.max(jnp.where(valid[:, None] > 0, denom, 0.0)) / (LENGTH * HEAD_DIM)
        return (totals, (result.astype(jnp.bfloat16), stream_grad.astype(jnp.bfloat16), peak))
    zeros = tuple((jnp.zeros_like(item) for item in params))
    sums, (outputs, grads, peaks) = lax.scan(per_image, zeros, (tokens, cotangent, limits))
    return (outputs, grads, jnp.max(peaks), sums[0], sums[1], sums[2], sums[3], sums[4], sums[5], sums[6], sums[7], sums[8], sums[9], sums[10], sums[11], sums[12], sums[13], sums[14], sums[15])
```

```python
import functools

import jax
import jax.numpy as jnp
from jax import lax
from jax.experimental import pallas as pl
from jax.experimental.pallas import tpu as pltpu
from jax.sharding import PartitionSpec as P

HEADS = 8
LEN_LONG = 3072
LEN_SHORT = 784
EPSILON = 1e-05
F32, BF16 = jnp.float32, jnp.bfloat16
MESH = pl.DeviceIdType.MESH

WIDTH = 512
PART = 512
QUAD = 256
DEPTH = 64
HALVINGS = 3
CHUNK = 1024
CHUNKS = 6
LANDS = 5
SHARES = (4, 3, 1)
VECS = 16
FIRST_LIMIT = 16


def mm(a, b):
    return lax.dot_general(a, b, (((1,), (0,)), ((), ())), preferred_element_type=F32)


def nt(a, b):
    return lax.dot_general(a, b, (((1,), (1,)), ((), ())), preferred_element_type=F32)


def tn(a, b):
    return lax.dot_general(a, b, (((0,), (0,)), ((), ())), preferred_element_type=F32)


def colsum(v):
    return jnp.sum(v, axis=0, keepdims=True)


def bit(index, step):
    return lax.rem(lax.div(index, step), 2)


def aligned(v, m=8):
    return v if isinstance(v, int) else pl.multiple_of(v, m)


def coord(dim):
    return bit(lax.axis_index(dim[0]), dim[1])


def peer(dim):
    axis, step = dim
    d, s = lax.axis_index("dp"), lax.axis_index("seq")
    if axis == "dp":
        return (d + step * (1 - 2 * bit(d, step)), s)
    return (d, s + step * (1 - 2 * bit(s, step)))


def remote(src, dst, send, recv, device):
    return pltpu.make_async_remote_copy(
        src_ref=src, dst_ref=dst, send_sem=send, recv_sem=recv, device_id=device, device_id_type=MESH
    )


class Reduce:
    def __init__(self, dims, orders):
        self.core, self.orders = ("dp", 1), orders
        self.half = CHUNK // 2
        unit = self.half // sum(SHARES)
        self.sizes = [unit * s for s in SHARES]
        self.starts = [sum(self.sizes[:i]) for i in range(len(SHARES))]
        self.whole = len(dims) - HALVINGS
        self.between = 2 * HALVINGS + self.whole
        self.steps = self.between + 3
        self.sems = 2 + len(SHARES) * self.between
        self.frees = 1 + len(SHARES) * HALVINGS
        self.bases = [self.half]
        for p in range(len(SHARES)):
            self.bases.append(self.bases[-1] + self.offset(p, HALVINGS + self.whole))
        self.rows = self.bases[-1]

    def offset(self, p, k):
        n = self.sizes[p]
        over = max(k - HALVINGS, 0)
        return n - (n >> min(k, HALVINGS)) + over * (n >> HALVINGS)

    def piece(self, p, k):
        at = coord(self.core) * self.half + self.starts[p]
        for i in range(k):
            at = at + coord(self.orders[p][i]) * (self.sizes[p] >> (i + 1))
        return at

    def copies(self, g, r, ss, rs, stage):
        half = self.half
        if stage in (0, self.steps - 2):
            c = coord(self.core)
            mine, other = aligned(c * half), aligned((1 - c) * half)
            if stage == 0:
                dst = r.at[pl.ds(0, half)]
                cp = remote(g.at[pl.ds(other, half)], dst, ss.at[0], rs.at[0], peer(self.core))
                return [(cp, mine, 0, half, 0, peer(self.core))]
            part = g.at[pl.ds(mine, half)]
            cp = remote(part, part, ss.at[1], rs.at[1], peer(self.core))
            return [(cp, None, None, half, 0, peer(self.core))]
        out = []
        k = stage - 1
        for p, order in enumerate(self.orders):
            n = self.sizes[p]
            sem = 2 + p * self.between + k
            land = self.bases[p] + self.offset(p, k)
            free = None
            if k < HALVINGS:
                free = 1 + p * HALVINGS + k
                m, dim, base = n >> (k + 1), order[k], self.piece(p, k)
                c = coord(dim)
                src = g.at[pl.ds(aligned(base + (1 - c) * m), m)]
                dst, to = r.at[pl.ds(land, m)], aligned(base + c * m)
            elif k < HALVINGS + self.whole:
                m, dim, to = n >> HALVINGS, order[k], aligned(self.piece(p, HALVINGS))
                src, dst = g.at[pl.ds(to, m)], r.at[pl.ds(land, m)]
            else:
                i = self.between - 1 - k
                free = 1 + p * HALVINGS + i
                m, dim, to, land = n >> (i + 1), order[i], None, None
                src = dst = g.at[pl.ds(aligned(self.piece(p, i + 1)), m)]
            cp = remote(src, dst, ss.at[sem], rs.at[sem], peer(dim))
            out.append((cp, to, land, m, free, peer(dim)))
        return out

    def step(self, g, r, ss, rs, fs, k):
        if k > 0:
            for cp, to, land, m, free, device in self.copies(g, r, ss, rs, k - 1):
                cp.wait()
                if to is not None:
                    slab = next(s for s in (64, 48, 32, 24, 16, 8) if m % s == 0)

                    def one(i, c, to=to, land=land, slab=slab):
                        a = pl.ds(pl.multiple_of(to + i * slab, 8), slab)
                        g[a, :] += r[pl.ds(pl.multiple_of(land + i * slab, 8), slab), :]
                        return c

                    lax.fori_loop(0, m // slab, one, 0)
                    if free is not None:
                        pl.semaphore_signal(fs.at[free], inc=1, device_id=device, device_id_type=MESH)
        if k < self.steps - 1:
            for cp, to, _, _, free, _ in self.copies(g, r, ss, rs, k):
                if to is None:
                    pl.semaphore_wait(fs.at[free], 1)
                cp.start()


class Scan:
    def __init__(self, seq, back, own, rx1, rxp, txp, tx2, rx2, prior, ss, rs):
        self.hops = seq // 2
        place = lax.axis_index("seq")
        self.dp, self.place = lax.axis_index("dp"), place
        lo, hi = lax.rem(place, 2), lax.div(place, 2)
        self.partner = (self.dp, place + 1 - 2 * lo)
        self.next = (self.dp, place - 2 if back else place + 2)
        self.lo = 1 - lo if back else lo
        self.hi = self.hops - 1 - hi if back else hi
        self.own, self.rx1, self.rxp, self.txp = own, rx1, rxp, txp
        self.tx2, self.rx2, self.prior, self.ss, self.rs = tx2, rx2, prior, ss, rs

    def first(self, b):
        src = self.own.at[b, 1 - self.lo]
        return remote(src, self.rx1.at[b], self.ss.at[b, 0], self.rs.at[b, 0], self.partner)

    def chain(self, b):
        return remote(
            self.txp.at[b], self.rxp.at[b], self.ss.at[b, 1], self.rs.at[b, 1], self.next
        )

    def last(self, b):
        return remote(
            self.tx2.at[b], self.rx2.at[b], self.ss.at[b, 2], self.rs.at[b, 2], self.partner
        )

    def begin(self, b):
        self.first(b).start()

    def hop(self, b):
        @pl.when(self.hi == 0)
        def _():
            self.rxp[b] = jnp.zeros_like(self.rxp[b])

        self.first(b).wait()
        mine = self.own[b, self.lo]
        other = self.rx1[b]

        @pl.when(self.hi > 0)
        def _():
            self.chain(b).wait_recv()

        came = self.rxp[b]

        @pl.when(self.hi < self.hops - 1)
        def _():
            self.txp[b] = came + mine + other
            self.chain(b).start()

        upper = self.lo.astype(F32)
        self.tx2[b] = came + (1.0 - upper) * mine
        self.last(b).start()
        self.prior[b, self.lo] = came + upper * other

    def end(self, b):
        self.last(b).wait()

        @pl.when(self.hi < self.hops - 1)
        def _():
            self.chain(b).wait_send()

        self.prior[b, 1 - self.lo] = self.rx2[b]


def norm_parts(v):
    centre = v - jnp.mean(v, axis=-1, keepdims=True)
    rate = lax.rsqrt(jnp.mean(centre * centre, axis=-1, keepdims=True) + EPSILON)
    return centre * rate, rate


def norm_back(grad, unit, rate, gain):
    inner = grad * gain
    shift = jnp.mean(inner, axis=-1, keepdims=True)
    scale = jnp.mean(inner * unit, axis=-1, keepdims=True)
    return rate * (inner - shift - unit * scale)


def feature(v):
    return jnp.where(v > 0, v + 1.0, jnp.exp(jnp.minimum(v, 0.0)))


def normal_parts(u):
    e = jnp.exp(-0.5 * u * u)
    t = 1.0 / (1.0 + 0.3275911 * 0.7071067811865476 * jnp.abs(u))
    poly = 1.421413741 + t * (-1.453152027 + t * 1.061405429)
    poly = t * (0.254829592 + t * (-0.284496736 + t * poly))
    tail = 0.5 * poly * e
    return jnp.where(u > 0, 1.0 - tail, tail), e * 0.3989422804014327


def split(v):
    high = v.astype(BF16)
    return high, (v - high.astype(F32)).astype(BF16)


def four(v):
    return jnp.concatenate([v] * 4, axis=0)


def fold(v):
    return v[0:64] + v[64:128] + v[128:192] + v[192:256]


N1G, N1B, QB, KB, VB, OB, N2G, N2B, RB, HB, PEAK = range(11)
PEAK = 13


def kernel(
    seq,
    images,
    span,
    red,
    dims,
    tok_hbm,
    cot_hbm,
    vec,
    wq_hbm,
    wk_hbm,
    wv_hbm,
    wo_hbm,
    w1_hbm,
    w2_hbm,
    lay_hbm,
    ing_hbm,
    gw2_hbm,
    gw1_hbm,
    gwo_hbm,
    gwq_hbm,
    gwk_hbm,
    gwv_hbm,
    sums_ref,
    x,
    ct,
    fq,
    fk,
    vb,
    at,
    iv,
    si,
    out,
    d2,
    ws,
    w1,
    w2,
    g,
    sb,
    srx,
    own,
    rx1,
    f_rxp,
    b_rxp,
    txp,
    tx2,
    rx2,
    f_prior,
    b_prior,
    mu,
    mx,
    bo,
    bof,
    cm,
    cmt,
    in_sem,
    w_sem,
    out_sem,
    go_sem,
    red_ss,
    red_rs,
    red_fs,
    f_ss,
    f_rs,
    b_ss,
    b_rs,
    s_ss,
    s_rs,
):
    per = 2 if images % 2 == 0 else 1
    blocks = images // per
    rows = per * span
    size = 128 if span % 128 == 0 else span
    parts = span // size
    place = lax.axis_index("seq")

    def block(b):
        return pl.ds(pl.multiple_of(b * rows, 16), rows)

    def image(b, im):
        return pl.ds(pl.multiple_of(b * rows + im * span, 16), span)

    def spot(b, im, c):
        return pl.ds(pl.multiple_of(b * rows + im * span + c * size, 16), size)

    def fetch(hbm, ref, sem, b):
        return pltpu.make_async_copy(hbm.at[block(b)], ref.at[block(b)], sem.at[b])

    for b in range(blocks):
        fetch(tok_hbm, x, in_sem.at[0], b).start()
    loads = [pltpu.make_async_copy(h, ws.at[i], w_sem.at[i]) for i, h in enumerate((wq_hbm, wk_hbm, wv_hbm, wo_hbm))]
    def weights(j):
        cols = pl.ds(j * PART, PART)
        return (
            pltpu.make_async_copy(w1_hbm.at[:, cols], w1.at[j % 2], w_sem.at[4 + j]),
            pltpu.make_async_copy(w2_hbm.at[cols, :], w2.at[j % 2], w_sem.at[8 + j]),
        )

    def fill(j):
        for load in weights(j):
            load.start()

    def filled(j):
        for load in weights(j):
            load.wait()

    for load in loads:
        load.start()
    fill(0)
    fill(1)
    for b in range(blocks):
        fetch(cot_hbm, ct, in_sem.at[1], b).start()

    barrier = pltpu.get_barrier_semaphore()
    chain = [(lax.axis_index("dp"), lax.rem(place + d, seq)) for d in (2, seq - 2)]
    friends = [peer(d) for d in [("dp", 1)] + dims] + chain
    for friend in friends:
        pl.semaphore_signal(barrier, inc=1, device_id=friend, device_id_type=MESH)

    same = lax.broadcasted_iota(jnp.int32, (QUAD, QUAD), 0) // DEPTH == lax.broadcasted_iota(jnp.int32, (QUAD, QUAD), 1) // DEPTH
    bof[...] = jnp.where(same, 1.0, 0.0)
    bo[...] = bof[...].astype(BF16)
    same = lax.broadcasted_iota(jnp.int32, (4 * size, QUAD), 0) // size == lax.broadcasted_iota(jnp.int32, (4 * size, QUAD), 1) // DEPTH
    mx[...] = jnp.where(same, 1.0, 0.0).astype(BF16)
    t = lax.broadcasted_iota(jnp.int32, (size, 4 * size), 0)
    s = lax.broadcasted_iota(jnp.int32, (size, 4 * size), 1) % size
    cm[...] = jnp.where(s <= t, 1.0, 0.0)
    cmt[...] = jnp.where(s >= t, 1.0, 0.0)
    sb[...] = jnp.zeros_like(sb)

    def clear(i, c):
        def inner(k, c):
            g[i, pl.ds(pl.multiple_of(k * 64, 8), 64), :] = jnp.zeros((64, WIDTH), F32)
            return c

        return lax.fori_loop(0, CHUNK // 64, inner, c)

    lax.fori_loop(0, LANDS, clear, 0)

    def row(i):
        return vec[i : i + 1, :]

    def add(i, v):
        sb[i : i + 1, :] += v

    def limit(b, im):
        return vec[pl.ds(FIRST_LIMIT + b * per + im, 1), :]

    def positions(start, count, width):
        return (lax.broadcasted_iota(jnp.int32, (count, width), 0) + (place * span + start)).astype(F32)

    forward = Scan(seq, False, own, rx1, f_rxp, txp, tx2, rx2, f_prior, f_ss, f_rs)
    backward = Scan(seq, True, own, rx1, b_rxp, txp, tx2, rx2, b_prior, b_ss, b_rs)

    for i in range(3):
        loads[i].wait()

    def phase_a(b, c):
        fetch(tok_hbm, x, in_sem.at[0], b).wait()
        pos = positions(0, span, WIDTH)
        for im in range(per):
            part = image(b, im)
            unit, _ = norm_parts(x[part, :].astype(F32))
            first = (unit * row(N1G) + row(N1B)).astype(BF16)
            fq[part, :] = feature(mm(first, ws[0]) + row(QB)).astype(BF16)
            key = feature(mm(first, ws[1]) + row(KB))
            key = jnp.where(pos < limit(b, im), key, 0.0).astype(BF16)
            fk[part, :] = key
            value = (mm(first, ws[2]) + row(VB)).astype(BF16)
            vb[part, :] = value
            total = colsum(key.astype(F32))
            for q in range(2):
                cols = slice(q * QUAD, (q + 1) * QUAD)
                state = fold(tn(key[:, cols], value[:, cols]) * bof[...])
                own[b, q, im * 64 : im * 64 + 64, :] = state
                own[b, q, per * 64 + im : per * 64 + im + 1, :] = total[:, cols]

        @pl.when(b == 0)
        def _():
            pl.semaphore_wait(barrier, len(friends))

        forward.begin(b)
        return c

    for q in range(2):
        for b in range(blocks):
            own[b, q, per * 64 : per * 64 + 8, :] = jnp.zeros((8, QUAD), F32)
    lax.fori_loop(0, blocks, phase_a, 0)

    def hops(scan):
        def one(b, c):
            scan.hop(b)
            return c

        lax.fori_loop(0, blocks, one, 0)

    hops(forward)
    loads[3].wait()
    filled(0)

    def known(ref, b, im, q):
        state = ref[b, q, pl.ds(pl.multiple_of(im * 64, 8), 64), :]
        return four(state) * bof[...], ref[b, q, pl.ds(per * 64 + im, 1), :]

    def entering(b, im, q):
        cols = slice(q * QUAD, (q + 1) * QUAD)
        state, total = known(f_prior, b, im, q)
        states, totals = [], []
        for c in range(parts):
            states.append(split(state))
            totals.append(total)
            if c < parts - 1:
                key = fk[spot(b, im, c), cols]
                state = state + tn(key, vb[spot(b, im, c), cols]) * bof[...]
                total = total + colsum(key.astype(F32))
        return states, totals

    def each(im, q):
        return [(im, q, c) for c in range(parts)]

    def read(ref, b, one):
        im, q, c = one
        return ref[spot(b, im, c), q * QUAD : (q + 1) * QUAD]

    def write(ref, b, one, v):
        im, q, c = one
        ref[spot(b, im, c), q * QUAD : (q + 1) * QUAD] = v

    def centre(b, im, q):
        return mu[pl.ds(b * per + im, 1), q * QUAD : (q + 1) * QUAD]

    def head_sums(v):
        high, low = split(v)
        return mm(high, bo[...]) + mm(low, bo[...])

    def attend(b, im):
        for q in range(2):
            near = pl.ds(pl.multiple_of(im * 64, 8), 64)
            count = f_prior[b, q, pl.ds(per * 64 + im, 1), :] + own[b, q, pl.ds(per * 64 + im, 1), :]
            count = head_sums(jnp.broadcast_to(count, (8, QUAD)))[0:1]
            off = colsum(f_prior[b, q, near, :] + own[b, q, near, :]) / count
            mu[pl.ds(b * per + im, 1), q * QUAD : (q + 1) * QUAD] = off
            ones = each(im, q)
            states, totals = entering(b, im, q)
            query = [read(fq, b, o) for o in ones]
            score = [(nt(u, four(read(fk, b, o)) * mx[...]) * cm[...]).astype(BF16) for u, o in zip(query, ones)]
            num = [mm(v, four(read(vb, b, o)) * mx[...]) for v, o in zip(score, ones)]
            den = [mm(v, mx[...]) for v in score]
            cols = slice(q * QUAD, (q + 1) * QUAD)
            for c, o in enumerate(ones):
                n = num[c] + mm(query[c], states[c][0]) + mm(query[c], states[c][1])
                d = den[c] + head_sums(query[c].astype(F32) * totals[c])
                inverse = 1.0 / d
                write(at, b, o, (n * inverse - off).astype(BF16))
                write(iv, b, o, inverse.astype(BF16))
                inside = positions(c * size, size, QUAD) < limit(b, im)[:, cols]
                peak = jnp.max(jnp.where(inside, d, 0.0), axis=0, keepdims=True)
                sb[PEAK : PEAK + 1, cols] = jnp.maximum(sb[PEAK : PEAK + 1, cols], peak)

    def uncentred(den_grad, num_grad, off):
        return den_grad.astype(F32) - head_sums(num_grad.astype(F32) * off)

    def attended(b, im):
        return (at[image(b, im), :].astype(F32) + mu[pl.ds(b * per + im, 1), :]).astype(BF16)

    def feed(j, b):
        normed, grad = si[block(b), :], ct[block(b), :]
        up, down = w1[lax.rem(j, 2)], w2[lax.rem(j, 2)]
        act, pre = [], []
        for im in range(per):
            part = slice(im * span, (im + 1) * span)
            hidden = mm(normed[part], up) + vec[pl.ds(HB + j, 1), :]
            back = nt(grad[part], down)
            cdf, pdf = normal_parts(hidden)
            act.append((hidden * cdf).astype(BF16))
            pre.append((back * (cdf + hidden * pdf)).astype(BF16))
            out[image(b, im), :] += mm(act[im], down)
            d2[image(b, im), :] += nt(pre[im], up)
        act, pre = jnp.concatenate(act, axis=0), jnp.concatenate(pre, axis=0)
        g[j, 0:512, :] += tn(act, grad)
        g[j, 512:1024, :] += tn(normed, pre)
        sb[pl.ds(HB + j, 1), :] += colsum(pre.astype(F32))

    def store(c, i):
        if i == 0:
            return pltpu.make_async_copy(g.at[c, pl.ds(0, 512)], gw2_hbm.at[pl.ds(pl.multiple_of(c * PART, PART), PART), :], go_sem.at[c, 0])
        return pltpu.make_async_copy(g.at[c, pl.ds(512, 512)], gw1_hbm.at[:, pl.ds(pl.multiple_of(c * PART, PART), PART)], go_sem.at[c, 1])

    times = red_times(red.steps)

    def tick(t):
        for k in reversed(range(red.steps)):
            ahead = t - times[k]
            c = lax.div(ahead, 3)

            @pl.when(jnp.logical_and(ahead >= 0, jnp.logical_and(lax.rem(ahead, 3) == 0, c < 4)))
            def _(k=k, c=c):
                red.step(g.at[c], g.at[LANDS + c], red_ss.at[c], red_rs.at[c], red_fs.at[c], k)
                if k == red.steps - 1:
                    store(c, 0).start()
                    store(c, 1).start()

    def phase_b(b, c):
        forward.end(b)
        def one(im, c):
            attend(b, im)
            return c

        lax.fori_loop(0, per, one, 0)
        for im in range(per):
            part = image(b, im)
            mid = x[part, :].astype(F32) + mm(attended(b, im), ws[3]) + row(OB)
            unit, _ = norm_parts(mid)
            si[part, :] = (unit * row(N2G) + row(N2B)).astype(BF16)
            out[part, :] = mid + row(RB)
        d2[block(b), :] = jnp.zeros((rows, WIDTH), F32)
        fetch(cot_hbm, ct, in_sem.at[1], b).wait()
        add(RB, colsum(ct[block(b), :].astype(F32)))
        feed(0, b)

        @pl.when(b == blocks - 1)
        def _():
            tick(0)

        return c

    lax.fori_loop(0, blocks, phase_b, 0)

    fill(2)
    filled(1)

    def phase_f(i, c):
        feed(1 + lax.div(i, blocks), lax.rem(i, blocks))

        @pl.when(i == blocks - 1)
        def _():
            fill(3)
            filled(2)

        tick(1 + i)
        return c

    lax.fori_loop(0, 2 * blocks, phase_f, 0)
    filled(3)
    tick0 = 1 + 2 * blocks

    def save(ref, hbm, b):
        return pltpu.make_async_copy(ref.at[block(b)], hbm.at[block(b)], out_sem.at[b])

    def phase_g(b, c):
        feed(3, b)
        def one(im, c):
            part = image(b, im)
            attn = attended(b, im)
            unit, rate = norm_parts(x[part, :].astype(F32) + mm(attn, ws[3]) + row(OB))
            grad = d2[part, :]
            add(N2G, colsum(grad * unit))
            add(N2B, colsum(grad))
            residual = ct[part, :].astype(F32) + norm_back(grad, unit, rate, row(N2G))
            d2[part, :] = residual
            ct[part, :] = out[part, :].astype(BF16)
            low = residual.astype(BF16)
            g[4, 0:512, :] += tn(attn, low)
            add(OB, colsum(low.astype(F32)))
            mixed_grad = nt(low, ws[3])
            inverse = iv[part, :].astype(F32)
            num_grad = (mixed_grad * inverse).astype(BF16)
            si[part, :] = num_grad
            inner = num_grad.astype(F32) * at[part, :].astype(F32)
            query = fq[part, :]
            for q in range(2):
                cols = slice(q * QUAD, (q + 1) * QUAD)
                den_grad = (-head_sums(inner[:, cols])).astype(BF16)
                iv[part, cols] = den_grad
                whole = uncentred(den_grad, num_grad[:, cols], centre(b, im, q))
                total = colsum(whole * query[:, cols].astype(F32))
                state = fold(tn(query[:, cols], num_grad[:, cols]) * bof[...])
                own[b, q, pl.ds(pl.multiple_of(im * 64, 8), 64), :] = state
                own[b, q, pl.ds(per * 64 + im, 1), :] = total
            return c

        lax.fori_loop(0, per, one, 0)
        save(ct, lay_hbm, b).start()
        backward.begin(b)
        tick(tick0 + b)
        return c

    lax.fori_loop(0, blocks, phase_g, 0)
    tick1 = tick0 + blocks

    @pl.when(backward.hi == 0)
    def _():
        hops(backward)

    def together(pieces):
        return jnp.concatenate([jnp.concatenate(p, axis=0) for p in pieces], axis=1)

    def less(b, one):
        return (read(vb, b, one).astype(F32) - centre(b, one[0], one[1])).astype(BF16)

    def query_side(b, im):
        unit, _ = norm_parts(x[image(b, im), :].astype(F32))
        first = (unit * row(N1G) + row(N1B)).astype(BF16)
        at[image(b, im), :] = first
        low = []
        for q in range(2):
            ones = each(im, q)
            states, totals = entering(b, im, q)
            num_grad = [read(si, b, o) for o in ones]
            den_grad = [read(iv, b, o) for o in ones]
            back = [
                ((nt(n, four(less(b, o)) * mx[...]) + nt(d, mx[...] * 0.015625)) * cm[...]).astype(BF16)
                for n, d, o in zip(num_grad, den_grad, ones)
            ]
            side = [mm(v, four(read(fk, b, o)) * mx[...]) for v, o in zip(back, ones)]
            pieces = []
            for c, o in enumerate(ones):
                whole = uncentred(den_grad[c], num_grad[c], centre(b, im, q))
                grad = side[c] + nt(num_grad[c], states[c][0]) + nt(num_grad[c], states[c][1])
                grad = grad + whole * totals[c]
                pieces.append((grad * jnp.minimum(read(fq, b, o).astype(F32), 1.0)).astype(BF16))
            low.append(pieces)
        low = together(low)
        g[4, 512:1024, :] += tn(first, low)
        add(QB, colsum(low.astype(F32)))
        out[image(b, im), :] = nt(low, ws[0])

    def phase_q(b, c):
        def one(im, c):
            query_side(b, im)
            return c

        lax.fori_loop(0, per, one, 0)
        due = jnp.logical_or(backward.hi == b + 1, jnp.logical_and(b == blocks - 1, backward.hi > blocks))

        @pl.when(due)
        def _():
            hops(backward)

        tick(tick1 + b)
        return c

    lax.fori_loop(0, blocks, phase_q, 0)
    tick2 = tick1 + blocks

    def chunk4(k):
        red.step(g.at[4], g.at[LANDS + 1], red_ss.at[1], red_rs.at[1], red_fs.at[1], k)

    def chunk5(k):
        red.step(g.at[5], g.at[LANDS + 2], red_ss.at[2], red_rs.at[2], red_fs.at[2], k)

    def key_side(b, im):
        first = at[image(b, im), :]
        share = jnp.full((size, QUAD), 0.015625, BF16)
        low_k, low_v = [], []
        for q in range(2):
            ones = each(im, q)
            cols = slice(q * QUAD, (q + 1) * QUAD)
            state, total = known(b_prior, b, im, q)
            states, totals = [], []
            for c in reversed(range(parts)):
                states.insert(0, split(state))
                totals.insert(0, total)
                if c > 0:
                    query, num_grad = fq[spot(b, im, c), cols], si[spot(b, im, c), cols]
                    state = state + tn(query, num_grad) * bof[...]
                    whole = uncentred(iv[spot(b, im, c), cols], num_grad, centre(b, im, q))
                    total = total + colsum(whole * query.astype(F32))
            spread_query = [four(read(fq, b, o)) * mx[...] for o in ones]
            spread_num = [four(read(si, b, o)) * mx[...] for o in ones]
            key = [read(fk, b, o) for o in ones]
            value = [read(vb, b, o) for o in ones]
            score = [(nt(k, s) * cmt[...]).astype(BF16) for k, s in zip(key, spread_query)]
            value_part = [mm(v, s) for v, s in zip(score, spread_num)]
            back = [
                ((nt(v, s) + nt(share, four(read(iv, b, o)) * mx[...])) * cmt[...]).astype(BF16)
                for v, s, o in zip([less(b, o) for o in ones], spread_num, ones)
            ]
            key_part = [mm(v, s) for v, s in zip(back, spread_query)]
            pieces_k, pieces_v = [], []
            for c in range(parts):
                grad = key_part[c] + nt(value[c], states[c][0]) + nt(value[c], states[c][1]) + totals[c]
                pieces_k.append((grad * jnp.minimum(key[c].astype(F32), 1.0)).astype(BF16))
                pieces_v.append((value_part[c] + mm(key[c], states[c][0])).astype(BF16))
            low_k.append(pieces_k)
            low_v.append(pieces_v)
        low_k, low_v = together(low_k), together(low_v)
        g[5, 0:512, :] += tn(first, low_k)
        g[5, 512:1024, :] += tn(first, low_v)
        add(KB, colsum(low_k.astype(F32)))
        add(VB, colsum(low_v.astype(F32)))
        out[image(b, im), :] += nt(low_k, ws[1]) + nt(low_v, ws[2])

    def phase_k(b, c):
        backward.end(b)

        def one(im, c):
            key_side(b, im)
            return c

        lax.fori_loop(0, per, one, 0)
        tick(tick2 + b)
        return c

    clear(CHUNKS - 1, 0)
    lax.fori_loop(0, blocks, phase_k, 0)
    tick3 = tick2 + blocks
    last = times[-1] + 9

    def drain(t, c):
        tick(t)
        return c

    def phase_n(b, c):
        for im in range(per):
            part = image(b, im)
            unit, rate = norm_parts(x[part, :].astype(F32))
            grad = out[part, :]
            add(N1G, colsum(grad * unit))
            add(N1B, colsum(grad))
            x[part, :] = (d2[part, :] + norm_back(grad, unit, rate, row(N1G))).astype(BF16)
        save(ct, lay_hbm, b).wait()
        save(x, ing_hbm, b).start()
        tick(tick3 + b)
        return c

    lax.fori_loop(0, blocks, phase_n, 0)
    lax.fori_loop(tick3 + blocks, last + 1, drain, 0)

    small = [("dp", 1)] + dims

    def swap(i):
        return remote(sb, srx.at[i], s_ss.at[i], s_rs.at[i], peer(small[i]))

    peaks = lax.broadcasted_iota(jnp.int32, (VECS, WIDTH), 0) == PEAK
    for k in range(max(red.steps + 1, len(small) + 1)):
        if k < red.steps:
            chunk4(k)
        if 1 <= k < red.steps + 1:
            chunk5(k - 1)
        if 0 < k <= len(small):
            swap(k - 1).wait()
            came = srx[k - 1]
            sb[...] = jnp.where(peaks, jnp.maximum(sb[...], came), sb[...] + came)
        if k < len(small):
            swap(k).start()
    tail = [
        pltpu.make_async_copy(g.at[4 + i // 2, pl.ds((i % 2) * 512, 512)], h, go_sem.at[4 + i // 2, i % 2])
        for i, h in enumerate((gwo_hbm, gwq_hbm, gwk_hbm, gwv_hbm))
    ]
    for copy in tail:
        copy.start()
    sums_ref[...] = sb[...]
    for b in range(blocks):
        save(x, ing_hbm, b).wait()
    for c in range(4):
        store(c, 0).wait()
        store(c, 1).wait()
    for copy in tail:
        copy.wait()


def red_times(steps):
    gaps = [0, 1, 3, 2] + [1] * (steps - 8) + [1, 1, 2, 1]
    total, times = 0, []
    for gap in gaps:
        total += gap
        times.append(total)
    return times


def per_device(
    seq,
    dp,
    tokens,
    short_counts,
    norm1_gain,
    norm1_bias,
    query_weight,
    query_bias,
    key_weight,
    key_bias,
    value_weight,
    value_bias,
    output_weight,
    output_bias,
    norm2_gain,
    norm2_bias,
    hidden_weight,
    hidden_bias,
    return_weight,
    return_bias,
    cotangent,
):
    images, span, width = tokens.shape
    flat = images * span
    per = 2 if images % 2 == 0 else 1
    blocks, rows = images // per, per * span
    size = 128 if span % 128 == 0 else span
    dims = [("dp", 1 << k) for k in range(1, dp.bit_length() - 1)]
    dims = dims + [("seq", 1 << k) for k in range(seq.bit_length() - 1)]
    turn = (len(dims) - 1) // 3
    orders = [dims[i * turn :] + dims[: i * turn] for i in range(3)]
    red = Reduce(dims, orders)
    limits = jnp.where(jnp.arange(images) < short_counts[0], LEN_SHORT, LEN_LONG).astype(F32)
    small = (norm1_gain, norm1_bias, query_bias, key_bias, value_bias, output_bias, norm2_gain, norm2_bias, return_bias)
    vec = jnp.concatenate(
        [v.astype(F32)[None] for v in small]
        + [hidden_bias.astype(F32).reshape(4, width), jnp.zeros((FIRST_LIMIT - 13, width), F32)]
        + [jnp.broadcast_to(limits[:, None], (images, width))],
        axis=0,
    )
    hbm = pl.BlockSpec(memory_space=pl.ANY)
    vmem = pl.BlockSpec(memory_space=pltpu.VMEM)
    unit = per * 64 + 8
    state = (blocks, unit, QUAD)
    big = lambda kind: pltpu.VMEM((flat, width), kind)
    f32 = lambda *shape: pltpu.VMEM(shape, F32)
    sem = lambda *shape: pltpu.SemaphoreType.DMA(shape)
    scratch = (
        [big(BF16)] * 8
        + [big(F32)] * 2
        + [pltpu.VMEM((4, width, width), BF16)]
        + [pltpu.VMEM((2, width, PART), BF16), pltpu.VMEM((2, PART, width), BF16)]
        + [f32(LANDS + 4, max(CHUNK, red.rows), width)]
        + [f32(VECS, width), f32(len(dims) + 1, VECS, width)]
        + [f32(blocks, 2, unit, QUAD)]
        + [f32(*state)] * 6
        + [f32(blocks, 2, unit, QUAD)] * 2
        + [f32(-(-images // 8) * 8, width)]
        + [pltpu.VMEM((4 * size, QUAD), BF16), pltpu.VMEM((QUAD, QUAD), BF16), f32(QUAD, QUAD)]
        + [f32(size, 4 * size)] * 2
        + [sem(2, blocks), sem(12), sem(blocks), sem(CHUNKS, 2)]
        + [sem(4, red.sems)] * 2
        + [pltpu.SemaphoreType.REGULAR((4, red.frees))]
        + [sem(blocks, 3)] * 4
        + [sem(len(dims) + 1)] * 2
    )
    shape = jax.ShapeDtypeStruct
    square = shape((width, width), F32)
    outs = pl.pallas_call(
        functools.partial(kernel, seq, images, span, red, dims),
        out_shape=(
            shape((flat, width), BF16),
            shape((flat, width), BF16),
            shape(return_weight.shape, F32),
            shape(hidden_weight.shape, F32),
            square,
            square,
            square,
            square,
            shape((VECS, width), F32),
        ),
        in_specs=[hbm, hbm, vmem] + [hbm] * 6,
        out_specs=(hbm,) * 8 + (vmem,),
        scratch_shapes=scratch,
        compiler_params=pltpu.CompilerParams(
            collective_id=0, has_side_effects=True, vmem_limit_bytes=63 * 2**20
        ),
    )(
        tokens.reshape(flat, width),
        cotangent.reshape(flat, width),
        vec,
        query_weight,
        key_weight,
        value_weight,
        output_weight,
        hidden_weight,
        return_weight,
    )
    lay, ing, gw2, gw1, gwo, gwq, gwk, gwv, sums = outs
    peak = jnp.max(sums[PEAK]) / (span * seq * (width // HEADS))
    return (
        lay.reshape(images, span, width),
        ing.reshape(images, span, width),
        peak,
        sums[N1G],
        sums[N1B],
        gwq,
        sums[QB],
        gwk,
        sums[KB],
        gwv,
        sums[VB],
        gwo,
        sums[OB],
        sums[N2G],
        sums[N2B],
        gw1,
        sums[HB : HB + 4].reshape(-1),
        gw2,
        sums[RB],
    )


def solution(mesh):
    split = P("dp", "seq", None)
    return jax.shard_map(
        functools.partial(per_device, mesh.shape["seq"], mesh.shape["dp"]),
        mesh=mesh,
        in_specs=(split, P("dp")) + (P(),) * 16 + (split,),
        out_specs=(split, split) + (P(),) * 17,
        check_vma=False,
    )
```

```python
import functools

import jax
import jax.numpy as jnp
from jax import lax
from jax.experimental import pallas as pl
from jax.experimental.pallas import tpu as pltpu
from jax.sharding import PartitionSpec as P

HEADS = 8
LEN_LONG = 3072
LEN_SHORT = 784
EPSILON = 1e-05
F32, BF16 = jnp.float32, jnp.bfloat16
MESH = pl.DeviceIdType.MESH

WIDTH = 512
PART = 512
QUAD = 256
DEPTH = 64
HALVINGS = 3
CHUNK = 1024
CHUNKS = 6
LANDS = 5
SHARES = (4, 3, 1)
VECS = 16


def mm(a, b):
    return lax.dot_general(a, b, (((1,), (0,)), ((), ())), preferred_element_type=F32)


def nt(a, b):
    return lax.dot_general(a, b, (((1,), (1,)), ((), ())), preferred_element_type=F32)


def tn(a, b):
    return lax.dot_general(a, b, (((0,), (0,)), ((), ())), preferred_element_type=F32)


def colsum(v):
    return jnp.sum(v, axis=0, keepdims=True)


def bit(index, step):
    return lax.rem(lax.div(index, step), 2)


def aligned(v, m=8):
    return v if isinstance(v, int) else pl.multiple_of(v, m)


def coord(dim):
    return bit(lax.axis_index(dim[0]), dim[1])


def peer(dim):
    axis, step = dim
    d, s = lax.axis_index("dp"), lax.axis_index("seq")
    if axis == "dp":
        return (d + step * (1 - 2 * bit(d, step)), s)
    return (d, s + step * (1 - 2 * bit(s, step)))


def remote(src, dst, send, recv, device):
    return pltpu.make_async_remote_copy(
        src_ref=src, dst_ref=dst, send_sem=send, recv_sem=recv, device_id=device, device_id_type=MESH
    )


class Reduce:
    def __init__(self, dims, orders):
        self.core, self.orders = ("dp", 1), orders
        self.half = CHUNK // 2
        unit = self.half // sum(SHARES)
        self.sizes = [unit * s for s in SHARES]
        self.starts = [sum(self.sizes[:i]) for i in range(len(SHARES))]
        self.whole = len(dims) - HALVINGS
        self.between = 2 * HALVINGS + self.whole
        self.steps = self.between + 3
        self.sems = 2 + len(SHARES) * self.between
        self.frees = 1 + len(SHARES) * (HALVINGS + self.whole)
        self.turn = HALVINGS + self.whole + 1
        self.bases = [self.half]
        for p in range(len(SHARES)):
            self.bases.append(self.bases[-1] + self.offset(p, HALVINGS + self.whole))
        self.rows = self.bases[-1]

    def offset(self, p, k):
        n = self.sizes[p]
        over = max(k - HALVINGS, 0)
        return n - (n >> min(k, HALVINGS)) + over * (n >> HALVINGS)

    def piece(self, p, k):
        at = coord(self.core) * self.half + self.starts[p]
        for i in range(k):
            at = at + coord(self.orders[p][i]) * (self.sizes[p] >> (i + 1))
        return at

    def copies(self, g, r, ss, rs, stage):
        half = self.half
        if stage in (0, self.steps - 2):
            c = coord(self.core)
            mine, other = aligned(c * half), aligned((1 - c) * half)
            if stage == 0:
                dst = r.at[pl.ds(0, half)]
                cp = remote(g.at[pl.ds(other, half)], dst, ss.at[0], rs.at[0], peer(self.core))
                return [(cp, mine, 0, half, 0, peer(self.core))]
            part = g.at[pl.ds(mine, half)]
            cp = remote(part, part, ss.at[1], rs.at[1], peer(self.core))
            return [(cp, None, None, half, None, peer(self.core))]
        out = []
        k = stage - 1
        for p, order in enumerate(self.orders):
            n = self.sizes[p]
            sem = 2 + p * self.between + k
            land = self.bases[p] + self.offset(p, k)
            free = 1 + p * (HALVINGS + self.whole) + k
            if k < HALVINGS:
                m, dim, base = n >> (k + 1), order[k], self.piece(p, k)
                c = coord(dim)
                src = g.at[pl.ds(aligned(base + (1 - c) * m), m)]
                dst, to = r.at[pl.ds(land, m)], aligned(base + c * m)
            elif k < HALVINGS + self.whole:
                m, dim, to = n >> HALVINGS, order[k], aligned(self.piece(p, HALVINGS))
                src, dst = g.at[pl.ds(to, m)], r.at[pl.ds(land, m)]
            else:
                i = self.between - 1 - k
                free = None
                m, dim, to, land = n >> (i + 1), order[i], None, None
                src = dst = g.at[pl.ds(aligned(self.piece(p, i + 1)), m)]
            cp = remote(src, dst, ss.at[sem], rs.at[sem], peer(dim))
            out.append((cp, to, land, m, free, peer(dim)))
        return out

    def step(self, g, r, ss, rs, fs, k):
        if k > 0:
            for cp, to, land, m, free, device in self.copies(g, r, ss, rs, k - 1):
                cp.wait()
                if to is not None:
                    slab = next(s for s in (64, 48, 32, 24, 16, 8) if m % s == 0)

                    def one(i, c, to=to, land=land, slab=slab):
                        a = pl.ds(pl.multiple_of(to + i * slab, 8), slab)
                        g[a, :] += r[pl.ds(pl.multiple_of(land + i * slab, 8), slab), :]
                        return c

                    lax.fori_loop(0, m // slab, one, 0)
                    pl.semaphore_signal(fs.at[free], inc=1, device_id=device, device_id_type=MESH)
        for n in range(HALVINGS + 1 if k == self.turn else 0):
            self.freed(fs, n)
        for n in range(HALVINGS + 1, self.turn if k == self.turn + 1 else 0):
            self.freed(fs, n)
        if k < self.steps - 1:
            for cp, *_ in self.copies(g, r, ss, rs, k):
                cp.start()

    def freed(self, fs, stage):
        if stage == 0:
            pl.semaphore_wait(fs.at[0], 1)
        else:
            for p in range(len(SHARES)):
                pl.semaphore_wait(fs.at[1 + p * (HALVINGS + self.whole) + stage - 1], 1)


class Scan:
    def __init__(self, seq, back, own, rx1, rxp, txp, tx2, rx2, prior, ss, rs):
        self.hops = seq // 2
        place = lax.axis_index("seq")
        self.dp, self.place = lax.axis_index("dp"), place
        lo, hi = lax.rem(place, 2), lax.div(place, 2)
        self.partner = (self.dp, place + 1 - 2 * lo)
        self.next = (self.dp, place - 2 if back else place + 2)
        self.lo = 1 - lo if back else lo
        self.hi = self.hops - 1 - hi if back else hi
        self.own, self.rx1, self.rxp, self.txp = own, rx1, rxp, txp
        self.tx2, self.rx2, self.prior, self.ss, self.rs = tx2, rx2, prior, ss, rs

    def first(self, i):
        src = self.own.at[i, 1 - self.lo]
        return remote(src, self.rx1.at[i], self.ss.at[i, 0], self.rs.at[i, 0], self.partner)

    def chain(self, i):
        return remote(
            self.txp.at[i], self.rxp.at[i], self.ss.at[i, 1], self.rs.at[i, 1], self.next
        )

    def last(self, i):
        return remote(
            self.tx2.at[i], self.rx2.at[i], self.ss.at[i, 2], self.rs.at[i, 2], self.partner
        )

    def begin(self, i):
        self.first(i).start()

    def hop(self, i):
        @pl.when(self.hi == 0)
        def _():
            self.rxp[i] = jnp.zeros_like(self.rxp[i])

        self.first(i).wait()
        mine = self.own[i, self.lo]
        other = self.rx1[i]

        @pl.when(self.hi > 0)
        def _():
            self.chain(i).wait_recv()

        came = self.rxp[i]

        @pl.when(self.hi < self.hops - 1)
        def _():
            self.txp[i] = came + mine + other
            self.chain(i).start()

        upper = self.lo.astype(F32)
        self.tx2[i] = came + (1.0 - upper) * mine
        self.last(i).start()
        self.prior[i, self.lo] = came + upper * other

    def end(self, i):
        self.last(i).wait()

        @pl.when(self.hi < self.hops - 1)
        def _():
            self.chain(i).wait_send()

        self.prior[i, 1 - self.lo] = self.rx2[i]


def norm_parts(v):
    centre = v - jnp.mean(v, axis=-1, keepdims=True)
    rate = lax.rsqrt(jnp.mean(centre * centre, axis=-1, keepdims=True) + EPSILON)
    return centre * rate, rate


def norm_back(grad, unit, rate, gain):
    inner = grad * gain
    shift = jnp.mean(inner, axis=-1, keepdims=True)
    scale = jnp.mean(inner * unit, axis=-1, keepdims=True)
    return rate * (inner - shift - unit * scale)


def feature(v):
    return jnp.where(v > 0, v + 1.0, jnp.exp(jnp.minimum(v, 0.0)))


def normal_parts(u):
    e = jnp.exp(-0.5 * u * u)
    t = 1.0 / (1.0 + 0.3275911 * 0.7071067811865476 * jnp.abs(u))
    poly = 1.421413741 + t * (-1.453152027 + t * 1.061405429)
    poly = t * (0.254829592 + t * (-0.284496736 + t * poly))
    tail = 0.5 * poly * e
    return jnp.where(u > 0, 1.0 - tail, tail), e * 0.3989422804014327


def split(v):
    high = v.astype(BF16)
    return high, (v - high.astype(F32)).astype(BF16)


def four(v):
    return jnp.concatenate([v] * 4, axis=0)


def fold(v):
    return v[0:64] + v[64:128] + v[128:192] + v[192:256]


def spread(v):
    inside = lax.broadcasted_iota(jnp.int32, (v.shape[0], 128), 1) < DEPTH
    out = []
    for t in range(2):
        tile = v[:, t * 128 : (t + 1) * 128]
        turned = pltpu.roll(tile, DEPTH, 1)
        out += [jnp.where(inside, tile, turned), jnp.where(inside, turned, tile)]
    return out


N1G, N1B, QB, KB, VB, OB, N2G, N2B, RB, HB = range(10)
PEAK = 13


def kernel(
    seq,
    images,
    span,
    red,
    dims,
    tok_hbm,
    cot_hbm,
    short_ref,
    vec_refs,
    wq_hbm,
    wk_hbm,
    wv_hbm,
    wo_hbm,
    w1_hbm,
    w2_hbm,
    lay_hbm,
    ing_hbm,
    gw2_hbm,
    gw1_hbm,
    gwo_hbm,
    gwq_hbm,
    gwk_hbm,
    gwv_hbm,
    sums_ref,
    x,
    ct,
    fq,
    fk,
    vb,
    at,
    iv,
    si,
    out,
    d2,
    ws,
    w1,
    w2,
    g,
    vec,
    sb,
    srx,
    own,
    rx1,
    f_rxp,
    b_rxp,
    txp,
    tx2,
    rx2,
    f_prior,
    b_prior,
    mu,
    dgt,
    gsum,
    mx,
    bo,
    bof,
    cm,
    cmt,
    in_sem,
    w_sem,
    out_sem,
    go_sem,
    red_ss,
    red_rs,
    red_fs,
    f_ss,
    f_rs,
    b_ss,
    b_rs,
    s_ss,
    s_rs,
):
    per = 2 if images % 2 == 0 else 1
    blocks = images // per
    rows = per * span
    size = 128 if span % 128 == 0 else span
    parts = span // size
    place = lax.axis_index("seq")
    small = [("dp", 1)] + dims

    step_s = images
    step_b = step_s + images
    step_f = step_b + 2 * blocks
    step_g = step_f + 2 * blocks
    step_q = step_g + 2 * blocks
    step_k = step_q + images
    step_n = step_k + images
    step_d = step_n + blocks
    times = red_times(red.steps)
    starts = [step_f - 1, step_f + blocks - 1, step_g - 1, step_q - 2]
    starts.append(max(step_k - 1, starts[1] + times[red.turn + 1]))
    starts.append(max(step_n - 1, starts[2] + times[red.turn + 1]))
    total_steps = max(starts[-1] + times[-1], step_d + len(small)) + 1

    def image(i):
        return pl.ds(pl.multiple_of(i * span, 16), span)

    def block(b):
        return pl.ds(pl.multiple_of(b * rows, 16), rows)

    def spot(i, c):
        return pl.ds(pl.multiple_of(i * span + c * size, 16), size)

    def fetch(hbm, ref, sem, i):
        return pltpu.make_async_copy(hbm.at[image(i)], ref.at[image(i)], sem.at[i])

    def save(ref, hbm, b):
        return pltpu.make_async_copy(ref.at[block(b)], hbm.at[block(b)], out_sem.at[b])

    fetch(tok_hbm, x, in_sem.at[0], 0).start()
    loads = [
        pltpu.make_async_copy(h, ws.at[i], w_sem.at[i])
        for i, h in enumerate((wq_hbm, wk_hbm, wv_hbm, wo_hbm))
    ]
    for load in loads[:3]:
        load.start()
    for i in range(1, images):
        fetch(tok_hbm, x, in_sem.at[0], i).start()
    loads[3].start()

    def weights(j):
        cols = pl.ds(j * PART, PART)
        return (
            pltpu.make_async_copy(w1_hbm.at[:, cols], w1.at[j % 2], w_sem.at[4 + j]),
            pltpu.make_async_copy(w2_hbm.at[cols, :], w2.at[j % 2], w_sem.at[8 + j]),
        )

    def fill(j):
        for load in weights(j):
            load.start()

    def filled(j):
        for load in weights(j):
            load.wait()

    fill(0)
    fill(1)
    for i in range(images):
        fetch(cot_hbm, ct, in_sem.at[1], i).start()

    barrier = pltpu.get_barrier_semaphore()
    chain = [(lax.axis_index("dp"), lax.rem(place + d, seq)) for d in (2, seq - 2)]
    friends = [peer(d) for d in small] + chain
    for friend in friends:
        pl.semaphore_signal(barrier, inc=1, device_id=friend, device_id_type=MESH)

    for i, ref in enumerate(vec_refs):
        vec[i : i + ref.shape[0] // WIDTH, :] = ref[...].astype(F32).reshape(-1, WIDTH)

    def iota(shape, axis):
        return lax.broadcasted_iota(jnp.int32, shape, axis)

    tile = (QUAD, QUAD)
    bof[...] = jnp.where(iota(tile, 0) // DEPTH == iota(tile, 1) // DEPTH, 1.0, 0.0)
    bo[...] = bof[...].astype(BF16)
    tall = (4 * size, QUAD)
    mx[...] = jnp.where(iota(tall, 0) // size == iota(tall, 1) // DEPTH, 1.0, 0.0).astype(BF16)
    wide = (size, 4 * size)
    cm[...] = jnp.where(iota(wide, 1) % size <= iota(wide, 0), 1.0, 0.0)
    cmt[...] = jnp.where(iota(wide, 1) % size >= iota(wide, 0), 1.0, 0.0)
    sb[...] = jnp.zeros_like(sb)

    def clear(c, ignored):
        def inner(k, ignored):
            g[c, pl.ds(pl.multiple_of(k * 64, 8), 64), :] = jnp.zeros((64, WIDTH), F32)
            return ignored

        return lax.fori_loop(0, CHUNK // 64, inner, ignored)

    def row(i):
        return vec[i : i + 1, :]

    def add(i, v):
        sb[i : i + 1, :] += v

    def limit(i):
        return jnp.where(i < short_ref[0], LEN_SHORT, LEN_LONG)

    def positions(start, count, width):
        return iota((count, width), 0) + (place * span + start)

    forward = Scan(seq, False, own, rx1, f_rxp, txp, tx2, rx2, f_prior, f_ss, f_rs)
    backward = Scan(seq, True, own, rx1, b_rxp, txp, tx2, rx2, b_prior, b_ss, b_rs)
    halves = [slice(q * QUAD, (q + 1) * QUAD) for q in range(2)]
    cells = [(q, c) for q in range(2) for c in range(parts)]

    def read(ref, i, q, c):
        return ref[spot(i, c), halves[q]]

    def together(pieces):
        rows_of = [jnp.concatenate(pieces[q * parts : (q + 1) * parts], axis=0) for q in range(2)]
        return jnp.concatenate(rows_of, axis=1)

    def put(i, q, state, total):
        own[i, q, 0:64, :] = fold(state)
        own[i, q, 64:65, :] = total

    def known(ref, i, q):
        return four(ref[i, q, 0:64, :]) * bof[...], ref[i, q, 64:65, :]

    def centre(i, q):
        return mu[pl.ds(i, 1), halves[q]]

    def head_sums(v):
        high, low = split(v)
        return mm(high, bo[...]) + mm(low, bo[...])

    def project(i):
        fetch(tok_hbm, x, in_sem.at[0], i).wait()

        @pl.when(i == 0)
        def _():
            for load in loads[:3]:
                load.wait()

        part = image(i)
        unit, _ = norm_parts(x[part, :].astype(F32))
        first = (unit * row(N1G) + row(N1B)).astype(BF16)
        key = feature(mm(first, ws[1]) + row(KB))
        inside = positions(0, span, WIDTH) < limit(i)
        key = jnp.where(inside, key, 0.0).astype(BF16)
        fk[part, :] = key
        value = (mm(first, ws[2]) + row(VB)).astype(BF16)
        vb[part, :] = value
        total = colsum(key.astype(F32))
        for q, cols in enumerate(halves):
            put(i, q, tn(key[:, cols], value[:, cols]) * bof[...], total[:, cols])
        fq[part, :] = feature(mm(first, ws[0]) + row(QB)).astype(BF16)

        @pl.when(i == 0)
        def _():
            pl.semaphore_wait(barrier, len(friends))

        forward.begin(i)

    def within(i):
        query = [read(fq, i, *o) for o in cells]
        score = [(nt(u, four(read(fk, i, *o)) * mx[...]) * cm[...]).astype(BF16) for u, o in zip(query, cells)]
        num = [mm(v, four(read(vb, i, *o)) * mx[...]) for v, o in zip(score, cells)]
        den = [mm(v, mx[...]) for v in score]
        for n, d, (q, c) in zip(num, den, cells):
            out[spot(i, c), halves[q]] = n
            d2[spot(i, c), halves[q]] = d

        @pl.when(i < LANDS)
        def _():
            clear(i, 0)

    def entering(i, q):
        state, total = known(f_prior, i, q)
        states, totals = [], []
        for c in range(parts):
            states.append(split(state))
            totals.append(total)
            if c < parts - 1:
                key = read(fk, i, q, c)
                state = state + tn(key, read(vb, i, q, c)) * bof[...]
                total = total + colsum(key.astype(F32))
        return states, totals

    def attend(i):
        forward.end(i)
        for q, cols in enumerate(halves):
            state, total = f_prior[i, q, 0:64, :], f_prior[i, q, 64:65, :]
            count = total + own[i, q, 64:65, :]
            count = head_sums(jnp.broadcast_to(count, (8, QUAD)))[0:1]
            off = colsum(state + own[i, q, 0:64, :]) / count
            mu[pl.ds(i, 1), cols] = off
        ahead = [entering(i, q) for q in range(2)]
        inside = positions(0, span, QUAD) < limit(i)
        for q, c in cells:
            at_spot = (spot(i, c), halves[q])
            query, off = fq[at_spot], centre(i, q)
            high, low = ahead[q][0][c]
            n = out[at_spot] + mm(query, high) + mm(query, low)
            d = d2[at_spot] + head_sums(query.astype(F32) * ahead[q][1][c])
            inverse = 1.0 / d
            at[at_spot] = (n * inverse - off).astype(BF16)
            iv[at_spot] = inverse.astype(BF16)
            peak = jnp.max(jnp.where(inside[c * size : (c + 1) * size], d, 0.0), axis=0, keepdims=True)
            sb[PEAK : PEAK + 1, halves[q]] = jnp.maximum(sb[PEAK : PEAK + 1, halves[q]], peak)
        part = image(i)
        mid = x[part, :].astype(F32) + mm(attended(i), ws[3]) + row(OB)
        unit, _ = norm_parts(mid)
        si[part, :] = (unit * row(N2G) + row(N2B)).astype(BF16)
        out[part, :] = mid + row(RB)
        d2[part, :] = jnp.zeros((span, WIDTH), F32)
        fetch(cot_hbm, ct, in_sem.at[1], i).wait()
        add(RB, colsum(ct[part, :].astype(F32)))

    def attended(i):
        return (at[image(i), :].astype(F32) + mu[pl.ds(i, 1), :]).astype(BF16)

    def feed(j, b):
        normed, grad = si[block(b), :], ct[block(b), :]
        up, down = w1[lax.rem(j, 2)], w2[lax.rem(j, 2)]
        act, pre = [], []
        for im in range(per):
            part = slice(im * span, (im + 1) * span)
            hidden = mm(normed[part], up) + vec[pl.ds(HB + j, 1), :]
            back = nt(grad[part], down)
            cdf, pdf = normal_parts(hidden)
            act.append((hidden * cdf).astype(BF16))
            pre.append((back * (cdf + hidden * pdf)).astype(BF16))
            out[image(b * per + im), :] += mm(act[im], down)
            d2[image(b * per + im), :] += nt(pre[im], up)
        act, pre = jnp.concatenate(act, axis=0), jnp.concatenate(pre, axis=0)
        g[j, 0:512, :] += tn(act, grad)
        g[j, 512:1024, :] += tn(normed, pre)
        sb[pl.ds(HB + j, 1), :] += colsum(pre.astype(F32))

    def norm_two(i):
        part = image(i)
        attn = attended(i)
        unit, rate = norm_parts(x[part, :].astype(F32) + mm(attn, ws[3]) + row(OB))
        grad = d2[part, :]
        add(N2G, colsum(grad * unit))
        add(N2B, colsum(grad))
        residual = ct[part, :].astype(F32) + norm_back(grad, unit, rate, row(N2G))
        d2[part, :] = residual
        ct[part, :] = out[part, :].astype(BF16)
        low = residual.astype(BF16)
        mixed_grad = nt(low, ws[3])
        inverse = iv[part, :].astype(F32)
        num_grad = (mixed_grad * inverse).astype(BF16)
        si[part, :] = num_grad
        inner = num_grad.astype(F32) * (at[part, :].astype(F32) + mu[pl.ds(i, 1), :])
        den_grad = jnp.concatenate([-head_sums(inner[:, cols]) for cols in halves], axis=1)
        high, low_part = split(den_grad)
        iv[part, :] = high
        at[part, :] = low_part
        query = fq[part, :]
        totals = den_grad * query.astype(F32)
        totals = [colsum(totals[c * size : (c + 1) * size]) for c in range(parts)]
        for c in range(1, parts):
            gsum[pl.ds(i * parts + c, 1), :] = totals[c]
        total = functools.reduce(lambda a, b: a + b, totals)
        for q, cols in enumerate(halves):
            put(i, q, tn(query[:, cols], num_grad[:, cols]) * bof[...], total[:, cols])
        backward.begin(i)
        pick = jnp.where(iota((8, WIDTH), 1) == iota((8, WIDTH), 0) * DEPTH, 1.0, 0.0).astype(BF16)
        dgt[i] = nt(pick, high) + nt(pick, low_part)
        g[4, 0:512, :] += tn(attn, low)
        add(OB, colsum(low.astype(F32)))

    def query_side(i):
        unit, _ = norm_parts(x[image(i), :].astype(F32))
        first = (unit * row(N1G) + row(N1B)).astype(BF16)
        ahead = [entering(i, q) for q in range(2)]
        num_grad = [read(si, i, *o) for o in cells]
        den_grad = [read(iv, i, *o).astype(F32) + read(at, i, *o).astype(F32) for o in cells]
        at[image(i), :] = first
        back = [nt(n, four(read(vb, i, *o)) * mx[...]) for n, o in zip(num_grad, cells)]
        back = [
            ((v + jnp.concatenate(spread_rows(d), axis=1)) * cm[...]).astype(BF16)
            for v, d in zip(back, den_grad)
        ]
        side = [mm(v, four(read(fk, i, *o)) * mx[...]) for v, o in zip(back, cells)]
        low = []
        for u, n, d, (q, c) in zip(side, num_grad, den_grad, cells):
            high, part = ahead[q][0][c]
            grad = u + nt(n, high) + nt(n, part) + d * ahead[q][1][c]
            low.append((grad * jnp.minimum(read(fq, i, q, c).astype(F32), 1.0)).astype(BF16))
        low = together(low)
        g[4, 512:1024, :] += tn(first, low)
        add(QB, colsum(low.astype(F32)))
        out[image(i), :] = nt(low, ws[0])

    def spread_rows(v):
        return [u[:, :size] for u in spread(v)]

    def key_side(i):
        backward.end(i)
        first = at[image(i), :]
        low_k, low_v = [], []
        for q in range(2):
            state, total = known(b_prior, i, q)
            states, totals = [], []
            for c in reversed(range(parts)):
                states.insert(0, split(state))
                totals.insert(0, total)
                if c > 0:
                    state = state + tn(read(fq, i, q, c), read(si, i, q, c)) * bof[...]
                    total = total + gsum[pl.ds(i * parts + c, 1), halves[q]]
            wide_query = [four(read(fq, i, q, c)) * mx[...] for c in range(parts)]
            wide_num = [four(read(si, i, q, c)) * mx[...] for c in range(parts)]
            key = [read(fk, i, q, c) for c in range(parts)]
            value = [read(vb, i, q, c) for c in range(parts)]
            score = [(nt(k, u) * cmt[...]).astype(BF16) for k, u in zip(key, wide_query)]
            value_part = [mm(v, u) for v, u in zip(score, wide_num)]
            back = []
            for c in range(parts):
                line = [dgt[i, 4 * q + h : 4 * q + h + 1, c * size : (c + 1) * size] for h in range(4)]
                line = jnp.concatenate(line, axis=1)
                back.append(((nt(value[c], wide_num[c]) + line) * cmt[...]).astype(BF16))
            key_part = [mm(v, u) for v, u in zip(back, wide_query)]
            for c in range(parts):
                (high, part), total = states[c], totals[c]
                grad = key_part[c] + nt(value[c], high) + nt(value[c], part) + total
                low_k.append((grad * jnp.minimum(key[c].astype(F32), 1.0)).astype(BF16))
                low_v.append((value_part[c] + mm(key[c], high)).astype(BF16))
        low_k, low_v = together(low_k), together(low_v)
        g[5, 0:512, :] += tn(first, low_k)
        g[5, 512:1024, :] += tn(first, low_v)
        add(KB, colsum(low_k.astype(F32)))
        add(VB, colsum(low_v.astype(F32)))
        out[image(i), :] += nt(low_k, ws[1]) + nt(low_v, ws[2])

    def norm_one(i):
        part = image(i)
        unit, rate = norm_parts(x[part, :].astype(F32))
        grad = out[part, :]
        add(N1G, colsum(grad * unit))
        add(N1B, colsum(grad))
        x[part, :] = (d2[part, :] + norm_back(grad, unit, rate, row(N1G))).astype(BF16)

    def over(body):
        def run(b):
            def one(im, ignored):
                body(b * per + im)
                return ignored

            lax.fori_loop(0, per, one, 0)

        return run

    def results(c):
        cols = pl.ds(pl.multiple_of(c * PART, PART), PART)
        two = [
            (c < 4, gw2_hbm.at[cols, :], gw1_hbm.at[:, cols]),
            (c == 4, gwo_hbm, gwq_hbm),
            (c == 5, gwk_hbm, gwv_hbm),
        ]
        upper, lower = g.at[c, pl.ds(0, 512)], g.at[c, pl.ds(512, 512)]
        return [
            (when, (pltpu.make_async_copy(upper, a, go_sem.at[c, 0]), pltpu.make_async_copy(lower, b, go_sem.at[c, 1])))
            for when, a, b in two
        ]

    def due(u):
        for k in reversed(range(red.steps)):
            c = -1
            for n, start in enumerate(starts):
                c = jnp.where(u == start + times[k], n, c)

            @pl.when(c >= 0)
            def _(k=k, c=c):
                land = LANDS + c - jnp.where(c >= 4, 3, 0)
                red.step(g.at[c], g.at[land], red_ss.at[c], red_rs.at[c], red_fs.at[c], k)
                if k == red.steps - 1:
                    for when, copies in results(c):

                        @pl.when(when)
                        def _(copies=copies):
                            for copy in copies:
                                copy.start()

    def swap(k):
        return remote(sb, srx.at[k], s_ss.at[k], s_rs.at[k], peer(small[k]))

    def swaps(u):
        peaks = iota((VECS, WIDTH), 0) == PEAK
        for k in range(len(small) + 1):

            @pl.when(u == step_d + k)
            def _(k=k):
                if k > 0:
                    swap(k - 1).wait()
                    came = srx[k - 1]
                    sb[...] = jnp.where(peaks, jnp.maximum(sb[...], came), sb[...] + came)
                if k < len(small):
                    swap(k).start()

    def hops(scan, start, stop):
        def one(i, ignored):
            scan.hop(i)
            return ignored

        lax.fori_loop(start, stop, one, 0)

    def ready(scan, begun, now, least):
        count = jnp.maximum(0, least)
        for i in range(images):
            arrived = begun[i] + 42 + 39 * scan.hi <= now
            count = jnp.maximum(count, jnp.where(arrived, i + 1, 0))
        return count

    opened = [13 * (i + 1) + 3 * i for i in range(images)]
    turned = [56 + 78 * (i // per) + 22 * (i % per) for i in range(images)]

    def forward_by(u):
        v = u - step_b
        late = 13 * step_b + 39 * v
        now = jnp.where(u < step_b, 13 * (u + 1), late)
        least = jnp.where(u < step_b, 0, per * (1 + lax.div(v, 2)))
        return ready(forward, opened, now, jnp.clip(least, 0, images))

    def hops_forward(u):
        hops(forward, jnp.where(u == 0, 0, forward_by(u - 1)), forward_by(u))

    def backward_by(u):
        v, w, y = u - step_g, u - step_q, u - step_k
        in_g = 78 * lax.div(v, 2) + jnp.where(lax.rem(v, 2) == 0, 34, 78)
        now = jnp.where(u < step_q, in_g, jnp.where(u < step_k, 78 * blocks + 24 * (w + 1), 78 * blocks + 24 * images + 33 * (y + 1)))
        least = jnp.clip(jnp.where(u < step_k - 1, 0, y + 2), 0, images)
        return ready(backward, turned, now - 20, least)

    def hops_backward(u):
        hops(backward, jnp.where(u == step_g, 0, backward_by(u - 1)), backward_by(u))

    def run(start, stop, body):
        def one(u, ignored):
            body(u)
            return ignored

        lax.fori_loop(start, stop, one, 0)

    def opening(u):
        @pl.when(u < step_s)
        def _():
            project(u)

        @pl.when(u >= step_s)
        def _():
            within(u - step_s)

        hops_forward(u)

    def part_first(u):
        b = lax.div(u - step_b, 2)
        hops_forward(u)

        @pl.when(lax.rem(u - step_b, 2) == 0)
        def _():
            over(attend)(b)

        @pl.when(lax.rem(u - step_b, 2) == 1)
        def _():
            feed(0, b)

    def part_between(u):
        @pl.when(u == step_f + blocks)
        def _():
            fill(3)
            filled(2)

        feed(1 + lax.div(u - step_f, blocks), lax.rem(u - step_f, blocks))
        due(u)

    def part_last(u):
        b = lax.div(u - step_g, 2)

        @pl.when(lax.rem(u - step_g, 2) == 0)
        def _():
            feed(3, b)

        @pl.when(lax.rem(u - step_g, 2) == 1)
        def _():
            over(norm_two)(b)
            save(ct, lay_hbm, b).start()

        due(u)
        hops_backward(u)

    def part_query(u):
        query_side(u - step_q)
        due(u)
        hops_backward(u)

    def part_key(u):
        key_side(u - step_k)
        due(u)
        hops_backward(u)

    def closing(u):
        @pl.when(u < step_d)
        def _():
            b = u - step_n
            over(norm_one)(b)
            save(ct, lay_hbm, b).wait()
            save(x, ing_hbm, b).start()

        due(u)
        swaps(u)

    run(0, step_b, opening)
    loads[3].wait()
    filled(0)
    run(step_b, step_f, part_first)
    due(step_f - 1)
    fill(2)
    filled(1)
    run(step_f, step_g, part_between)
    filled(3)
    run(step_g, step_q, part_last)
    run(step_q, step_k, part_query)
    clear(CHUNKS - 1, 0)
    run(step_k, step_n, part_key)
    run(step_n, total_steps, closing)
    sums_ref[...] = sb[...]
    for b in range(blocks):
        save(x, ing_hbm, b).wait()
    for c in range(CHUNKS):
        for copy in results(c)[max(c - 3, 0)][1]:
            copy.wait()


def deliver(scale, sums, *refs):
    big, (peak, hidden), vectors = refs[:8], refs[16:18], refs[18:-9]
    held, sems = refs[-9:-1], refs[-1]
    pieces = []
    for a, b, v in zip(big, refs[8:16], held):
        step = a.shape[0] // 4
        for n in range(4):
            part = pl.ds(n * step, step)
            k = len(pieces)
            pieces.append((pltpu.make_async_copy(a.at[part], v.at[part], sems.at[k, 0]), pltpu.make_async_copy(v.at[part], b.at[part], sems.at[k, 1])))
    for come, _ in pieces:
        come.start()
    peak[0] = jnp.max(sums[PEAK : PEAK + 1, :]) * scale
    hidden[...] = sums[HB : HB + 4, :].reshape(4 * WIDTH)
    for i, ref in enumerate(vectors):
        ref[...] = sums[i : i + 1, :].reshape(WIDTH)
    for come, go in pieces:
        come.wait()
        go.start()
    for _, go in pieces:
        go.wait()


def red_times(steps):
    gaps = [0, 2, 3, 3, 2] + [2] * (steps - 9) + [2, 3, 4, 2]
    total, times = 0, []
    for gap in gaps:
        total += gap
        times.append(total)
    return times


def per_device(
    seq,
    dp,
    tokens,
    short_counts,
    norm1_gain,
    norm1_bias,
    query_weight,
    query_bias,
    key_weight,
    key_bias,
    value_weight,
    value_bias,
    output_weight,
    output_bias,
    norm2_gain,
    norm2_bias,
    hidden_weight,
    hidden_bias,
    return_weight,
    return_bias,
    cotangent,
):
    images, span, width = tokens.shape
    flat = images * span
    per = 2 if images % 2 == 0 else 1
    blocks = images // per
    size = 128 if span % 128 == 0 else span
    dims = [("dp", 1 << k) for k in range(1, dp.bit_length() - 1)]
    dims = dims + [("seq", 1 << k) for k in range(seq.bit_length() - 1)]
    turn = (len(dims) - 1) // 3
    orders = [dims[i * turn :] + dims[: i * turn] for i in range(3)]
    red = Reduce(dims, orders)
    small = (norm1_gain, norm1_bias, query_bias, key_bias, value_bias, output_bias, norm2_gain, norm2_bias, return_bias)
    small = small + (hidden_bias,)
    hbm = pl.BlockSpec(memory_space=pl.ANY)
    vmem = pl.BlockSpec(memory_space=pltpu.VMEM)
    smem = pl.BlockSpec(memory_space=pltpu.SMEM)
    state = (images, 72, QUAD)
    pair = (images, 2, 72, QUAD)
    big = lambda kind: pltpu.VMEM((flat, width), kind)
    f32 = lambda *shape: pltpu.VMEM(shape, F32)
    sem = lambda *shape: pltpu.SemaphoreType.DMA(shape)
    scratch = (
        [big(BF16)] * 8
        + [big(F32)] * 2
        + [pltpu.VMEM((4, width, width), BF16)]
        + [pltpu.VMEM((2, width, PART), BF16), pltpu.VMEM((2, PART, width), BF16)]
        + [f32(LANDS + 4, max(CHUNK, red.rows), width)]
        + [f32(VECS, width)] * 2
        + [f32(len(dims) + 1, VECS, width)]
        + [f32(*pair)]
        + [f32(*state)] * 6
        + [f32(*pair)] * 2
        + [f32(-(-images // 8) * 8, width), f32(images, 8, span), f32(-(-images * (span // size) // 8) * 8, width)]
        + [pltpu.VMEM((4 * size, QUAD), BF16), pltpu.VMEM((QUAD, QUAD), BF16), f32(QUAD, QUAD)]
        + [f32(size, 4 * size)] * 2
        + [sem(2, images), sem(12), sem(blocks), sem(CHUNKS, 2)]
        + [sem(CHUNKS, red.sems)] * 2
        + [pltpu.SemaphoreType.REGULAR((CHUNKS, red.frees))]
        + [sem(images, 3)] * 4
        + [sem(len(dims) + 1)] * 2
    )
    shape = jax.ShapeDtypeStruct
    square = shape((width, width), F32)
    outs = pl.pallas_call(
        functools.partial(kernel, seq, images, span, red, dims),
        out_shape=(
            shape((flat, width), BF16),
            shape((flat, width), BF16),
            shape(return_weight.shape, F32),
            shape(hidden_weight.shape, F32),
            square,
            square,
            square,
            square,
            shape((VECS, width), F32),
        ),
        in_specs=[hbm, hbm, smem, (vmem,) * len(small)] + [hbm] * 6,
        out_specs=(hbm,) * 8 + (vmem,),
        scratch_shapes=scratch,
        compiler_params=pltpu.CompilerParams(
            collective_id=0, has_side_effects=True, vmem_limit_bytes=63 * 2**20
        ),
    )(
        tokens.reshape(flat, width),
        cotangent.reshape(flat, width),
        short_counts,
        small,
        query_weight,
        key_weight,
        value_weight,
        output_weight,
        hidden_weight,
        return_weight,
    )
    results, sums = outs[:8], outs[8]
    smalls = (shape((1,), F32), shape(hidden_bias.shape, F32)) + (shape((width,), F32),) * HB
    outs = pl.pallas_call(
        functools.partial(deliver, 1.0 / (span * seq * (width // HEADS))),
        out_shape=tuple(shape(v.shape, v.dtype) for v in results) + smalls,
        in_specs=[vmem] + [hbm] * 8,
        out_specs=(hbm,) * 8 + (smem,) + (vmem,) * (1 + HB),
        scratch_shapes=[pltpu.VMEM(v.shape, v.dtype) for v in results] + [sem(32, 2)],
        compiler_params=pltpu.CompilerParams(vmem_limit_bytes=63 * 2**20),
    )(sums, *results)
    lay, ing, gw2, gw1, gwo, gwq, gwk, gwv, peak, hidden = outs[:10]
    n1g, n1b, qb, kb, vb, ob, n2g, n2b, rb = outs[10:]
    lay, ing = lay.reshape(tokens.shape), ing.reshape(tokens.shape)
    attention = (gwq, qb, gwk, kb, gwv, vb, gwo, ob)
    return (lay, ing, peak.reshape(()), n1g, n1b) + attention + (n2g, n2b, gw1, hidden, gw2, rb)


def solution(mesh):
    split = P("dp", "seq", None)
    return jax.shard_map(
        functools.partial(per_device, mesh.shape["seq"], mesh.shape["dp"]),
        mesh=mesh,
        in_specs=(split, P("dp")) + (P(),) * 16 + (split,),
        out_specs=(split, split) + (P(),) * 17,
        check_vma=False,
    )
```

```python
import functools

import jax
import jax.numpy as jnp
from jax import lax
from jax.experimental import pallas as pl
from jax.experimental.pallas import tpu as pltpu
from jax.sharding import PartitionSpec as P

HEADS = 8
LEN_LONG = 3072
LEN_SHORT = 784
EPSILON = 1e-05
F32, BF16 = jnp.float32, jnp.bfloat16
MESH = pl.DeviceIdType.MESH

WIDTH = 512
PART = 512
QUAD = 256
DEPTH = 64
HALVINGS = 3
CHUNK = 1024
CHUNKS = 6
LANDS = 5
SHARES = (4, 3, 1)
LATE_SHARES = (2, 1, 1)
VECS = 16


def mm(a, b):
    return lax.dot_general(a, b, (((1,), (0,)), ((), ())), preferred_element_type=F32)


def nt(a, b):
    return lax.dot_general(a, b, (((1,), (1,)), ((), ())), preferred_element_type=F32)


def tn(a, b):
    return lax.dot_general(a, b, (((0,), (0,)), ((), ())), preferred_element_type=F32)


def colsum(v):
    return jnp.sum(v, axis=0, keepdims=True)


def bit(index, step):
    return lax.rem(lax.div(index, step), 2)


def aligned(v, m=8):
    return v if isinstance(v, int) else pl.multiple_of(v, m)


def coord(dim):
    return bit(lax.axis_index(dim[0]), dim[1])


def peer(dim):
    axis, step = dim
    d, s = lax.axis_index("dp"), lax.axis_index("seq")
    if axis == "dp":
        return (d + step * (1 - 2 * bit(d, step)), s)
    return (d, s + step * (1 - 2 * bit(s, step)))


def remote(src, dst, send, recv, device):
    return pltpu.make_async_remote_copy(
        src_ref=src, dst_ref=dst, send_sem=send, recv_sem=recv, device_id=device, device_id_type=MESH
    )


class Reduce:
    def __init__(self, dims, orders, rows, shares):
        self.core, self.orders = ("dp", 1), orders
        self.half = rows // 2
        unit = self.half // sum(shares)
        self.sizes = [unit * s for s in shares]
        self.starts = [sum(self.sizes[:i]) for i in range(len(shares))]
        self.whole = len(dims) - HALVINGS
        self.between = 2 * HALVINGS + self.whole
        self.steps = self.between + 3
        self.sems = 2 + len(shares) * self.between
        self.dims = [self.core] + dims
        self.frees = len(self.dims) + len(shares) * self.whole
        self.turn = HALVINGS + self.whole + 1
        self.bases = [self.half]
        for p in range(len(shares)):
            self.bases.append(self.bases[-1] + self.offset(p, HALVINGS + self.whole))
        self.rows = self.bases[-1]

    def enter(self):
        self.bits = {dim: coord(dim) for dim in self.dims}
        self.peers = {dim: peer(dim) for dim in self.dims}

    def offset(self, p, k):
        n = self.sizes[p]
        over = max(k - HALVINGS, 0)
        return n - (n >> min(k, HALVINGS)) + over * (n >> HALVINGS)

    def piece(self, p, k):
        at = self.bits[self.core] * self.half + self.starts[p]
        for i in range(k):
            at = at + self.bits[self.orders[p][i]] * (self.sizes[p] >> (i + 1))
        return at

    def copies(self, g, r, ss, rs, stage):
        half = self.half
        if stage in (0, self.steps - 2):
            c = self.bits[self.core]
            mine, other = aligned(c * half), aligned((1 - c) * half)
            if stage == 0:
                dst = r.at[pl.ds(0, half)]
                cp = remote(g.at[pl.ds(other, half)], dst, ss.at[0], rs.at[0], self.peers[self.core])
                return [(cp, mine, 0, half, None, None)]
            part = g.at[pl.ds(mine, half)]
            cp = remote(part, part, ss.at[1], rs.at[1], self.peers[self.core])
            return [(cp, None, None, half, None, None)]
        out = []
        k = stage - 1
        for p, order in enumerate(self.orders):
            n = self.sizes[p]
            sem = 2 + p * self.between + k
            land = self.bases[p] + self.offset(p, k)
            free = None
            if k < HALVINGS:
                m, dim, base = n >> (k + 1), order[k], self.piece(p, k)
                c = self.bits[dim]
                src = g.at[pl.ds(aligned(base + (1 - c) * m), m)]
                dst, to = r.at[pl.ds(land, m)], aligned(base + c * m)
            elif k < HALVINGS + self.whole:
                free = len(self.dims) + p * self.whole + k - HALVINGS
                m, dim, to = n >> HALVINGS, order[k], aligned(self.piece(p, HALVINGS))
                src, dst = g.at[pl.ds(to, m)], r.at[pl.ds(land, m)]
            else:
                i = self.between - 1 - k
                m, dim, to, land = n >> (i + 1), order[i], None, None
                src = dst = g.at[pl.ds(aligned(self.piece(p, i + 1)), m)]
            cp = remote(src, dst, ss.at[sem], rs.at[sem], self.peers[dim])
            out.append((cp, to, land, m, free, self.peers[dim]))
        return out

    def step(self, g, r, ss, rs, fs, k):
        if k > 0:
            for cp, to, land, m, free, device in self.copies(g, r, ss, rs, k - 1):
                cp.wait()
                if to is not None:
                    slab = next(s for s in (64, 48, 32, 24, 16, 8) if m % s == 0)

                    def one(i, c, to=to, land=land, slab=slab):
                        a = pl.ds(pl.multiple_of(to + i * slab, 8), slab)
                        g[a, :] += r[pl.ds(pl.multiple_of(land + i * slab, 8), slab), :]
                        return c

                    lax.fori_loop(0, m // slab, one, 0)
                    if free is not None:
                        pl.semaphore_signal(fs.at[free], inc=1, device_id=device, device_id_type=MESH)
        if k == HALVINGS + 1:
            for i, dim in enumerate(self.dims):
                pl.semaphore_signal(fs.at[i], inc=1, device_id=self.peers[dim], device_id_type=MESH)
        if k == self.turn:
            for i in range(len(self.dims)):
                pl.semaphore_wait(fs.at[i], 1)
        if k == self.turn + 1:
            for i in range(len(self.dims), self.frees):
                pl.semaphore_wait(fs.at[i], 1)
        if k < self.steps - 1:
            for cp, *_ in self.copies(g, r, ss, rs, k):
                cp.start()


class Scan:
    def __init__(self, seq, back, own, rx1, rxp, txp, tx2, rx2, prior, ss, rs):
        self.hops = seq // 2
        place = lax.axis_index("seq")
        self.dp, self.place = lax.axis_index("dp"), place
        lo, hi = lax.rem(place, 2), lax.div(place, 2)
        self.partner = (self.dp, place + 1 - 2 * lo)
        self.next = (self.dp, place - 2 if back else place + 2)
        self.lo = 1 - lo if back else lo
        self.hi = self.hops - 1 - hi if back else hi
        self.own, self.rx1, self.rxp, self.txp = own, rx1, rxp, txp
        self.tx2, self.rx2, self.prior, self.ss, self.rs = tx2, rx2, prior, ss, rs

    def first(self, i):
        src = self.own.at[i, 1 - self.lo]
        return remote(src, self.rx1.at[i], self.ss.at[i, 0], self.rs.at[i, 0], self.partner)

    def chain(self, i):
        return remote(
            self.txp.at[i], self.rxp.at[i], self.ss.at[i, 1], self.rs.at[i, 1], self.next
        )

    def last(self, i):
        return remote(
            self.tx2.at[i], self.rx2.at[i], self.ss.at[i, 2], self.rs.at[i, 2], self.partner
        )

    def begin(self, i):
        self.first(i).start()

    def hop(self, i):
        @pl.when(self.hi == 0)
        def _():
            self.rxp[i] = jnp.zeros_like(self.rxp[i])

        self.first(i).wait()
        mine = self.own[i, self.lo]
        other = self.rx1[i]

        @pl.when(self.hi > 0)
        def _():
            self.chain(i).wait_recv()

        came = self.rxp[i]

        @pl.when(self.hi < self.hops - 1)
        def _():
            self.txp[i] = came + mine + other
            self.chain(i).start()

        upper = self.lo.astype(F32)
        self.tx2[i] = came + (1.0 - upper) * mine
        self.last(i).start()
        self.prior[i, self.lo] = came + upper * other

    def end(self, i):
        self.last(i).wait()

        @pl.when(self.hi < self.hops - 1)
        def _():
            self.chain(i).wait_send()

        self.prior[i, 1 - self.lo] = self.rx2[i]


def norm_parts(v):
    centre = v - jnp.mean(v, axis=-1, keepdims=True)
    rate = lax.rsqrt(jnp.mean(centre * centre, axis=-1, keepdims=True) + EPSILON)
    return centre * rate, rate


def norm_back(grad, unit, rate, gain):
    inner = grad * gain
    shift = jnp.mean(inner, axis=-1, keepdims=True)
    scale = jnp.mean(inner * unit, axis=-1, keepdims=True)
    return rate * (inner - shift - unit * scale)


def feature(v):
    return jnp.where(v > 0, v + 1.0, jnp.exp(jnp.minimum(v, 0.0)))


def normal_parts(u):
    e = jnp.exp(-0.5 * u * u)
    t = 1.0 / (1.0 + 0.3275911 * 0.7071067811865476 * jnp.abs(u))
    poly = 1.421413741 + t * (-1.453152027 + t * 1.061405429)
    poly = t * (0.254829592 + t * (-0.284496736 + t * poly))
    tail = 0.5 * poly * e
    return jnp.where(u > 0, 1.0 - tail, tail), e * 0.3989422804014327


def split(v):
    high = v.astype(BF16)
    return high, (v - high.astype(F32)).astype(BF16)


def four(v):
    return jnp.concatenate([v] * 4, axis=0)


def fold(v):
    return v[0:64] + v[64:128] + v[128:192] + v[192:256]


def spread(v):
    inside = lax.broadcasted_iota(jnp.int32, (v.shape[0], 128), 1) < DEPTH
    out = []
    for t in range(2):
        tile = v[:, t * 128 : (t + 1) * 128]
        turned = pltpu.roll(tile, DEPTH, 1)
        out += [jnp.where(inside, tile, turned), jnp.where(inside, turned, tile)]
    return out


N1G, N1B, QB, KB, VB, OB, N2G, N2B, RB, HB = range(10)
PEAK = 13


def kernel(
    seq,
    images,
    span,
    red,
    late,
    dims,
    tok_hbm,
    cot_hbm,
    short_ref,
    vec_refs,
    wq_hbm,
    wk_hbm,
    wv_hbm,
    wo_hbm,
    w1_hbm,
    w2_hbm,
    x,
    ct,
    g,
    sums_ref,
    fq,
    fk,
    vb,
    at,
    iv,
    si,
    out,
    d2,
    ws,
    w1,
    w2,
    lands,
    vec,
    sb,
    srx,
    own,
    rx1,
    f_rxp,
    b_rxp,
    txp,
    tx2,
    rx2,
    f_prior,
    b_prior,
    mu,
    dgt,
    gsum,
    late_sums,
    mx,
    bo,
    bof,
    cm,
    cmt,
    in_sem,
    w_sem,
    red_ss,
    red_rs,
    red_fs,
    f_ss,
    f_rs,
    b_ss,
    b_rs,
    s_ss,
    s_rs,
):
    per = 2 if images % 2 == 0 else 1
    blocks = images // per
    rows = per * span
    size = 128 if span % 128 == 0 else span
    parts = span // size
    place = lax.axis_index("seq")
    small = [("dp", 1)] + dims
    red.enter()
    late.enter()

    step_s = images
    step_b = step_s + images
    step_f = step_b + 2 * blocks
    step_g = step_f + 2 * blocks
    step_q = step_g + 2 * blocks
    step_k = step_q + images
    step_n = step_k + 2 * images
    step_d = step_n + blocks
    spans = [13] * step_b + [35, 34] * blocks + [34] * (2 * blocks) + [34, 44] * blocks
    spans += [23] * images + [16] * (2 * images) + [11] * blocks
    clock = [sum(spans[: u + 1]) for u in range(len(spans))]
    clock += [clock[-1] + 20 * n for n in range(1, 80)]

    def places(start, offsets):
        return [next(u for u, t in enumerate(clock) if t >= clock[start] + d) for d in offsets]

    slow, fast = red_offsets(red, RED_GAPS), red_offsets(late, LATE_GAPS)
    when = [places(start, slow) for start in (step_f - 1, step_f + blocks - 1, step_g - 1, step_q - 2)]
    when.append(places(max(step_k - 1, when[1][red.turn + 1]), red_offsets(red, MID_GAPS)))
    when.append(places(max(step_k + images - 1, when[2][red.turn + 1]), fast))
    when.append(places(max(step_n - 1, when[2][red.turn + 1]), fast))
    total_steps = max([step_d + len(small)] + [places_of[-1] for places_of in when]) + 1

    def image(i):
        return pl.ds(pl.multiple_of(i * span, 16), span)

    def block(b):
        return pl.ds(pl.multiple_of(b * rows, 16), rows)

    def spot(i, c):
        return pl.ds(pl.multiple_of(i * span + c * size, 16), size)

    def fetch(hbm, ref, sem, i):
        return pltpu.make_async_copy(hbm.at[image(i)], ref.at[image(i)], sem.at[i])

    fetch(tok_hbm, x, in_sem.at[0], 0).start()
    loads = [
        pltpu.make_async_copy(h, ws.at[i], w_sem.at[i])
        for i, h in enumerate((wq_hbm, wk_hbm, wv_hbm, wo_hbm))
    ]
    for load in loads[:3]:
        load.start()
    for i in range(1, images):
        fetch(tok_hbm, x, in_sem.at[0], i).start()
    loads[3].start()

    def weights(j):
        cols = pl.ds(j * PART, PART)
        return (
            pltpu.make_async_copy(w1_hbm.at[:, cols], w1.at[j % 2], w_sem.at[4 + j]),
            pltpu.make_async_copy(w2_hbm.at[cols, :], w2.at[j % 2], w_sem.at[8 + j]),
        )

    def fill(j):
        for load in weights(j):
            load.start()

    def filled(j):
        for load in weights(j):
            load.wait()

    fill(0)
    fill(1)
    for i in range(images):
        fetch(cot_hbm, ct, in_sem.at[1], i).start()

    barrier = pltpu.get_barrier_semaphore()
    chain = [(lax.axis_index("dp"), lax.rem(place + d, seq)) for d in (2, seq - 2)]
    friends = [peer(d) for d in small] + chain
    for friend in friends:
        pl.semaphore_signal(barrier, inc=1, device_id=friend, device_id_type=MESH)

    for i, ref in enumerate(vec_refs):
        vec[i : i + ref.shape[0] // WIDTH, :] = ref[...].astype(F32).reshape(-1, WIDTH)

    def iota(shape, axis):
        return lax.broadcasted_iota(jnp.int32, shape, axis)

    tile = (QUAD, QUAD)
    bof[...] = jnp.where(iota(tile, 0) // DEPTH == iota(tile, 1) // DEPTH, 1.0, 0.0)
    bo[...] = bof[...].astype(BF16)
    tall = (4 * size, QUAD)
    mx[...] = jnp.where(iota(tall, 0) // size == iota(tall, 1) // DEPTH, 1.0, 0.0).astype(BF16)
    wide = (size, 4 * size)
    cm[...] = jnp.where(iota(wide, 1) % size <= iota(wide, 0), 1.0, 0.0)
    cmt[...] = jnp.where(iota(wide, 1) % size >= iota(wide, 0), 1.0, 0.0)
    sb[...] = jnp.zeros_like(sb)
    late_sums[...] = jnp.zeros_like(late_sums)

    def clear(c, ignored):
        def inner(k, ignored):
            g[c, pl.ds(pl.multiple_of(k * 64, 8), 64), :] = jnp.zeros((64, WIDTH), F32)
            return ignored

        return lax.fori_loop(0, CHUNK // 64, inner, ignored)

    def row(i):
        return vec[i : i + 1, :]

    def add(i, v):
        sb[i : i + 1, :] += v

    def limit(i):
        return jnp.where(i < short_ref[0], LEN_SHORT, LEN_LONG)

    def positions(start, count, width):
        return iota((count, width), 0) + (place * span + start)

    forward = Scan(seq, False, own, rx1, f_rxp, txp, tx2, rx2, f_prior, f_ss, f_rs)
    backward = Scan(seq, True, own, rx1, b_rxp, txp, tx2, rx2, b_prior, b_ss, b_rs)
    halves = [slice(q * QUAD, (q + 1) * QUAD) for q in range(2)]
    cells = [(q, c) for q in range(2) for c in range(parts)]

    def read(ref, i, q, c):
        return ref[spot(i, c), halves[q]]

    def together(pieces):
        rows_of = [jnp.concatenate(pieces[q * parts : (q + 1) * parts], axis=0) for q in range(2)]
        return jnp.concatenate(rows_of, axis=1)

    def put(i, q, state, total):
        own[i, q, 0:64, :] = fold(state)
        own[i, q, 64:65, :] = total

    def known(ref, i, q):
        return four(ref[i, q, 0:64, :]) * bof[...], ref[i, q, 64:65, :]

    def centre(i, q):
        return mu[pl.ds(i, 1), halves[q]]

    def head_sums(v):
        high, low = split(v)
        return mm(high, bo[...]) + mm(low, bo[...])

    def project(i):
        fetch(tok_hbm, x, in_sem.at[0], i).wait()

        @pl.when(i == 0)
        def _():
            for load in loads[:3]:
                load.wait()

        part = image(i)
        unit, _ = norm_parts(x[part, :].astype(F32))
        first = (unit * row(N1G) + row(N1B)).astype(BF16)
        key = feature(mm(first, ws[1]) + row(KB))
        inside = positions(0, span, WIDTH) < limit(i)
        key = jnp.where(inside, key, 0.0).astype(BF16)
        fk[part, :] = key
        value = (mm(first, ws[2]) + row(VB)).astype(BF16)
        vb[part, :] = value
        total = colsum(key.astype(F32))
        for q, cols in enumerate(halves):
            put(i, q, tn(key[:, cols], value[:, cols]) * bof[...], total[:, cols])
        fq[part, :] = feature(mm(first, ws[0]) + row(QB)).astype(BF16)

        @pl.when(i == 0)
        def _():
            pl.semaphore_wait(barrier, len(friends))

        forward.begin(i)

    def within(i):
        query = [read(fq, i, *o) for o in cells]
        score = [(nt(u, four(read(fk, i, *o)) * mx[...]) * cm[...]).astype(BF16) for u, o in zip(query, cells)]
        num = [mm(v, four(read(vb, i, *o)) * mx[...]) for v, o in zip(score, cells)]
        den = [mm(v, mx[...]) for v in score]
        for n, d, (q, c) in zip(num, den, cells):
            out[spot(i, c), halves[q]] = n
            d2[spot(i, c), halves[q]] = d

        @pl.when(i < LANDS)
        def _():
            clear(i, 0)

    def entering(i, q):
        state, total = known(f_prior, i, q)
        states, totals = [], []
        for c in range(parts):
            states.append(split(state))
            totals.append(total)
            if c < parts - 1:
                key = read(fk, i, q, c)
                state = state + tn(key, read(vb, i, q, c)) * bof[...]
                total = total + colsum(key.astype(F32))
        return states, totals

    def attend(i):
        forward.end(i)
        for q, cols in enumerate(halves):
            state, total = f_prior[i, q, 0:64, :], f_prior[i, q, 64:65, :]
            count = total + own[i, q, 64:65, :]
            count = head_sums(jnp.broadcast_to(count, (8, QUAD)))[0:1]
            off = colsum(state + own[i, q, 0:64, :]) / count
            mu[pl.ds(i, 1), cols] = off
        ahead = [entering(i, q) for q in range(2)]
        inside = positions(0, span, QUAD) < limit(i)
        for q, c in cells:
            at_spot = (spot(i, c), halves[q])
            query, off = fq[at_spot], centre(i, q)
            high, low = ahead[q][0][c]
            n = out[at_spot] + mm(query, high) + mm(query, low)
            d = d2[at_spot] + head_sums(query.astype(F32) * ahead[q][1][c])
            inverse = 1.0 / d
            at[at_spot] = (n * inverse - off).astype(BF16)
            iv[at_spot] = inverse.astype(BF16)
            peak = jnp.max(jnp.where(inside[c * size : (c + 1) * size], d, 0.0), axis=0, keepdims=True)
            sb[PEAK : PEAK + 1, halves[q]] = jnp.maximum(sb[PEAK : PEAK + 1, halves[q]], peak)
        part = image(i)
        mid = x[part, :].astype(F32) + mm(attended(i), ws[3]) + row(OB)
        unit, _ = norm_parts(mid)
        si[part, :] = (unit * row(N2G) + row(N2B)).astype(BF16)
        out[part, :] = mid + row(RB)
        d2[part, :] = jnp.zeros((span, WIDTH), F32)
        fetch(cot_hbm, ct, in_sem.at[1], i).wait()
        add(RB, colsum(ct[part, :].astype(F32)))

    def attended(i):
        return (at[image(i), :].astype(F32) + mu[pl.ds(i, 1), :]).astype(BF16)

    def feed(j, b):
        normed, grad = si[block(b), :], ct[block(b), :]
        up, down = w1[lax.rem(j, 2)], w2[lax.rem(j, 2)]
        act, pre = [], []
        for im in range(per):
            part = slice(im * span, (im + 1) * span)
            hidden = mm(normed[part], up) + vec[pl.ds(HB + j, 1), :]
            back = nt(grad[part], down)
            cdf, pdf = normal_parts(hidden)
            act.append((hidden * cdf).astype(BF16))
            pre.append((back * (cdf + hidden * pdf)).astype(BF16))
            out[image(b * per + im), :] += mm(act[im], down)
            d2[image(b * per + im), :] += nt(pre[im], up)
        act, pre = jnp.concatenate(act, axis=0), jnp.concatenate(pre, axis=0)
        g[j, 0:512, :] += tn(act, grad)
        g[j, 512:1024, :] += tn(normed, pre)
        sb[pl.ds(HB + j, 1), :] += colsum(pre.astype(F32))

    def norm_two(i):
        part = image(i)
        attn = attended(i)
        unit, rate = norm_parts(x[part, :].astype(F32) + mm(attn, ws[3]) + row(OB))
        grad = d2[part, :]
        add(N2G, colsum(grad * unit))
        add(N2B, colsum(grad))
        residual = ct[part, :].astype(F32) + norm_back(grad, unit, rate, row(N2G))
        d2[part, :] = residual
        ct[part, :] = out[part, :].astype(BF16)
        low = residual.astype(BF16)
        mixed_grad = nt(low, ws[3])
        inverse = iv[part, :].astype(F32)
        num_grad = (mixed_grad * inverse).astype(BF16)
        si[part, :] = num_grad
        inner = num_grad.astype(F32) * (at[part, :].astype(F32) + mu[pl.ds(i, 1), :])
        den_grad = jnp.concatenate([-head_sums(inner[:, cols]) for cols in halves], axis=1)
        high, low_part = split(den_grad)
        iv[part, :] = high
        at[part, :] = low_part
        query = fq[part, :]
        totals = den_grad * query.astype(F32)
        totals = [colsum(totals[c * size : (c + 1) * size]) for c in range(parts)]
        for c in range(1, parts):
            for q, cols in enumerate(halves):
                gsum[i * parts + c, q, 0:1, :] = totals[c][:, cols]
        total = functools.reduce(lambda a, b: a + b, totals)
        for q, cols in enumerate(halves):
            put(i, q, tn(query[:, cols], num_grad[:, cols]) * bof[...], total[:, cols])
        backward.begin(i)
        pick = jnp.where(iota((8, WIDTH), 1) == iota((8, WIDTH), 0) * DEPTH, 1.0, 0.0).astype(BF16)
        line = nt(pick, high) + nt(pick, low_part)
        dgt[i, 0, 0:4, :] = line[0:4]
        dgt[i, 1, 0:4, :] = line[4:8]
        g[4, 0:512, :] += tn(attn, low)
        add(OB, colsum(low.astype(F32)))

    def query_side(i):
        unit, _ = norm_parts(x[image(i), :].astype(F32))
        first = (unit * row(N1G) + row(N1B)).astype(BF16)
        ahead = [entering(i, q) for q in range(2)]
        num_grad = [read(si, i, *o) for o in cells]
        den_grad = [read(iv, i, *o).astype(F32) + read(at, i, *o).astype(F32) for o in cells]
        at[image(i), :] = first
        back = [nt(n, four(read(vb, i, *o)) * mx[...]) for n, o in zip(num_grad, cells)]
        back = [
            ((v + jnp.concatenate(spread_rows(d), axis=1)) * cm[...]).astype(BF16)
            for v, d in zip(back, den_grad)
        ]
        side = [mm(v, four(read(fk, i, *o)) * mx[...]) for v, o in zip(back, cells)]
        low = []
        for u, n, d, (q, c) in zip(side, num_grad, den_grad, cells):
            high, part = ahead[q][0][c]
            grad = u + nt(n, high) + nt(n, part) + d * ahead[q][1][c]
            low.append((grad * jnp.minimum(read(fq, i, q, c).astype(F32), 1.0)).astype(BF16))
        low = together(low)
        g[4, 512:1024, :] += tn(first, low)
        add(QB, colsum(low.astype(F32)))
        out[image(i), :] = nt(low, ws[0])

    def spread_rows(v):
        return [u[:, :size] for u in spread(v)]

    def key_side(i, q):
        cols = pl.ds(pl.multiple_of(q * QUAD, QUAD), QUAD)
        first = at[image(i), :]
        state, total = known(b_prior, i, q)
        states, totals = [], []
        for c in reversed(range(parts)):
            states.insert(0, split(state))
            totals.insert(0, total)
            if c > 0:
                state = state + tn(fq[spot(i, c), cols], si[spot(i, c), cols]) * bof[...]
                total = total + gsum[i * parts + c, q, 0:1, :]
        wide_query = [four(fq[spot(i, c), cols]) * mx[...] for c in range(parts)]
        wide_num = [four(si[spot(i, c), cols]) * mx[...] for c in range(parts)]
        key = [fk[spot(i, c), cols] for c in range(parts)]
        value = [vb[spot(i, c), cols] for c in range(parts)]
        score = [(nt(k, u) * cmt[...]).astype(BF16) for k, u in zip(key, wide_query)]
        value_part = [mm(v, u) for v, u in zip(score, wide_num)]
        back = []
        for c in range(parts):
            line = [dgt[i, q, h : h + 1, c * size : (c + 1) * size] for h in range(4)]
            line = jnp.concatenate(line, axis=1)
            back.append(((nt(value[c], wide_num[c]) + line) * cmt[...]).astype(BF16))
        key_part = [mm(v, u) for v, u in zip(back, wide_query)]
        low_k, low_v = [], []
        for c in range(parts):
            (high, part), total = states[c], totals[c]
            grad = key_part[c] + nt(value[c], high) + nt(value[c], part) + total
            low_k.append((grad * jnp.minimum(key[c].astype(F32), 1.0)).astype(BF16))
            low_v.append((value_part[c] + mm(key[c], high)).astype(BF16))
        low_k, low_v = jnp.concatenate(low_k, axis=0), jnp.concatenate(low_v, axis=0)
        both = jnp.concatenate([low_k, low_v], axis=1)
        g[5, pl.ds(pl.multiple_of(q * 512, 512), 512), :] += tn(first, both)
        late_sums[q, 0:1, :] += colsum(both.astype(F32))
        out[image(i), :] += nt(low_k, ws[1, :, cols]) + nt(low_v, ws[2, :, cols])

    def norm_one(i):
        part = image(i)
        unit, rate = norm_parts(x[part, :].astype(F32))
        grad = out[part, :]
        add(N1G, colsum(grad * unit))
        add(N1B, colsum(grad))
        x[part, :] = (d2[part, :] + norm_back(grad, unit, rate, row(N1G))).astype(BF16)

    def over(body):
        def run(b):
            def one(im, ignored):
                body(b * per + im)
                return ignored

            lax.fori_loop(0, per, one, 0)

        return run

    events = sorted((u, c, k) for c, line in enumerate(when) for k, u in enumerate(line))

    def advance(c, k):
        sems = (red_ss.at[c], red_rs.at[c], red_fs.at[c])
        if c < 5:
            land = g.at[CHUNKS - 1] if c == 0 else lands.at[c - 1 if c < 4 else 0]
            red.step(g.at[c], land, *sems, k)
        else:
            mine = g.at[5, pl.ds((c - 5) * 512, 512)]
            late.step(mine, lands.at[1, pl.ds((c - 5) * late.rows, late.rows)], *sems, k)

    def due(u, start, stop):
        for at_step, c, k in events:
            if isinstance(u, int):
                if at_step == u:
                    advance(c, k)
            elif start <= at_step < stop:

                @pl.when(u == at_step)
                def _(c=c, k=k):
                    advance(c, k)

    def swap(k):
        return remote(sb, srx.at[k], s_ss.at[k], s_rs.at[k], peer(small[k]))

    def swaps(u):
        peaks = iota((VECS, WIDTH), 0) == PEAK
        for k in range(len(small) + 1):

            if u == step_d + k:
                if k > 0:
                    swap(k - 1).wait()
                    came = srx[k - 1]
                    sb[...] = jnp.where(peaks, jnp.maximum(sb[...], came), sb[...] + came)
                if k < len(small):
                    swap(k).start()

    def hops(scan, start, stop):
        def one(i, ignored):
            scan.hop(i)
            return ignored

        lax.fori_loop(start, stop, one, 0)

    def ready(scan, begun, now, least):
        count = jnp.maximum(0, least)
        for i in range(images):
            arrived = begun[i] + 42 + 39 * scan.hi <= now
            count = jnp.maximum(count, jnp.where(arrived, i + 1, 0))
        return count

    opened = [13 * (i + 1) + 3 * i for i in range(images)]
    turned = [56 + 78 * (i // per) + 22 * (i % per) for i in range(images)]

    def forward_by(u):
        v = u - step_b
        late = 13 * step_b + 39 * v
        now = jnp.where(u < step_b, 13 * (u + 1), late)
        least = jnp.where(u < step_b, 0, per * (1 + lax.div(v, 2)))
        return ready(forward, opened, now, jnp.clip(least, 0, images))

    def hops_forward(u):
        hops(forward, jnp.where(u == 0, 0, forward_by(u - 1)), forward_by(u))

    def backward_by(u):
        v, w, y = u - step_g, u - step_q, u - step_k
        in_g = 78 * lax.div(v, 2) + jnp.where(lax.rem(v, 2) == 0, 34, 78)
        now = jnp.where(u < step_q, in_g, jnp.where(u < step_k, 78 * blocks + 24 * (w + 1), 78 * blocks + 24 * images + 17 * (y + 1)))
        least = jnp.clip(jnp.where(u < step_k - 1, 0, y + 2), 0, images)
        return ready(backward, turned, now - 20, least)

    def hops_backward(u):
        hops(backward, jnp.where(u == step_g, 0, backward_by(u - 1)), backward_by(u))

    def run(start, stop, body):
        def one(u, ignored):
            body(u)
            return ignored

        lax.fori_loop(start, stop, one, 0)

    def opening(u):
        @pl.when(u < step_s)
        def _():
            project(u)

        @pl.when(u >= step_s)
        def _():
            within(u - step_s)

        hops_forward(u)

    def part_first(u):
        b = lax.div(u - step_b, 2)
        hops_forward(u)

        @pl.when(lax.rem(u - step_b, 2) == 0)
        def _():
            over(attend)(b)

        @pl.when(lax.rem(u - step_b, 2) == 1)
        def _():
            feed(0, b)

    def part_between(u):
        @pl.when(u == step_f + blocks)
        def _():
            fill(3)
            filled(2)

        feed(1 + lax.div(u - step_f, blocks), lax.rem(u - step_f, blocks))
        due(u, step_f, step_g)

    def part_last(u):
        b = lax.div(u - step_g, 2)

        @pl.when(lax.rem(u - step_g, 2) == 0)
        def _():
            feed(3, b)

        @pl.when(lax.rem(u - step_g, 2) == 1)
        def _():
            over(norm_two)(b)

        due(u, step_g, step_q)
        hops_backward(u)

    def part_query(u):
        query_side(u - step_q)
        due(u, step_q, step_k)
        hops_backward(u)

    def part_key(u):
        i, q = lax.rem(u - step_k, images), lax.div(u - step_k, images)

        @pl.when(q == 0)
        def _():
            backward.end(i)

        key_side(i, q)
        due(u, step_k, step_n)
        hops_backward(u)

    def closing(u):
        if u < step_d:
            b = u - step_n
            over(norm_one)(b)
        due(u, u, u + 1)
        swaps(u)

    run(0, step_b, opening)
    loads[3].wait()
    filled(0)
    run(step_b, step_f, part_first)
    due(step_f - 1, 0, 0)
    fill(2)
    filled(1)
    run(step_f, step_g, part_between)
    filled(3)
    run(step_g, step_q, part_last)
    run(step_q, step_k, part_query)
    clear(CHUNKS - 1, 0)
    run(step_k, step_n, part_key)
    for q, cols in enumerate(halves):
        sb[KB : KB + 1, cols] = late_sums[q, 0:1, 0:QUAD]
        sb[VB : VB + 1, cols] = late_sums[q, 0:1, QUAD:WIDTH]
    for u in range(step_n, total_steps):
        closing(u)
    sums_ref[...] = sb[...]


def deliver(scale, ing, lay, g, sums, *refs):
    ing_out, lay_out, gw2, gw1, gwo, gwq, gwk, gwv, peak, hidden = refs[:10]
    sems = refs[-1]
    pairs = [(ing, ing_out), (lay, lay_out)]
    for c in range(4):
        cols = pl.ds(c * PART, PART)
        pairs += [(g.at[c, pl.ds(0, 512)], gw2.at[cols, :]), (g.at[c, pl.ds(512, 512)], gw1.at[:, cols])]
    pairs += [(g.at[4, pl.ds(0, 512)], gwo), (g.at[4, pl.ds(512, 512)], gwq)]
    for q in range(2):
        rows, cols = pl.ds(q * 512, 512), pl.ds(q * QUAD, QUAD)
        pairs += [
            (g.at[5, rows, pl.ds(0, QUAD)], gwk.at[:, cols]),
            (g.at[5, rows, pl.ds(QUAD, QUAD)], gwv.at[:, cols]),
        ]
    copies = [pltpu.make_async_copy(a, b, sems.at[i]) for i, (a, b) in enumerate(pairs)]
    for copy in copies:
        copy.start()
    peak[0] = jnp.max(sums[PEAK : PEAK + 1, :]) * scale
    hidden[...] = sums[HB : HB + 4, :].reshape(4 * WIDTH)
    for i, ref in enumerate(refs[10:-1]):
        ref[...] = sums[i : i + 1, :].reshape(WIDTH)
    for copy in copies:
        copy.wait()


RED_GAPS = (40, 100, 80, 60, 50, 50, 70, 100, 50)
MID_GAPS = (35, 80, 55, 45, 40, 40, 50, 80, 40)
LATE_GAPS = (30, 55, 40, 32, 32, 32, 40, 55, 30)


def red_offsets(red, gaps):
    gaps = gaps[:4] + gaps[4:5] * (red.steps - 9) + gaps[5:] if red.steps > 9 else gaps[: red.steps - 1]
    return [sum(gaps[:k]) for k in range(red.steps)]


def per_device(
    seq,
    dp,
    tokens,
    short_counts,
    norm1_gain,
    norm1_bias,
    query_weight,
    query_bias,
    key_weight,
    key_bias,
    value_weight,
    value_bias,
    output_weight,
    output_bias,
    norm2_gain,
    norm2_bias,
    hidden_weight,
    hidden_bias,
    return_weight,
    return_bias,
    cotangent,
):
    images, span, width = tokens.shape
    flat = images * span
    per = 2 if images % 2 == 0 else 1
    blocks = images // per
    size = 128 if span % 128 == 0 else span
    dims = [("dp", 1 << k) for k in range(1, dp.bit_length() - 1)]
    dims = dims + [("seq", 1 << k) for k in range(seq.bit_length() - 1)]
    turn = (len(dims) - 1) // 3
    orders = [dims[i * turn :] + dims[: i * turn] for i in range(3)]
    red = Reduce(dims, orders, CHUNK, SHARES)
    late = Reduce(dims, orders, CHUNK // 2, LATE_SHARES)
    small = (norm1_gain, norm1_bias, query_bias, key_bias, value_bias, output_bias, norm2_gain, norm2_bias, return_bias)
    small = small + (hidden_bias,)
    hbm = pl.BlockSpec(memory_space=pl.ANY)
    vmem = pl.BlockSpec(memory_space=pltpu.VMEM)
    smem = pl.BlockSpec(memory_space=pltpu.SMEM)
    state = (images, 72, QUAD)
    pair = (images, 2, 72, QUAD)
    big = lambda kind: pltpu.VMEM((flat, width), kind)
    f32 = lambda *shape: pltpu.VMEM(shape, F32)
    sem = lambda *shape: pltpu.SemaphoreType.DMA(shape)
    scratch = (
        [big(BF16)] * 6
        + [big(F32)] * 2
        + [pltpu.VMEM((4, width, width), BF16)]
        + [pltpu.VMEM((2, width, PART), BF16), pltpu.VMEM((2, PART, width), BF16)]
        + [f32(3, max(CHUNK, red.rows, 2 * late.rows), width)]
        + [f32(VECS, width)] * 2
        + [f32(len(dims) + 1, VECS, width)]
        + [f32(*pair)]
        + [f32(*state)] * 6
        + [f32(*pair)] * 2
        + [f32(-(-images // 8) * 8, width), f32(images, 2, 8, span), f32(images * (span // size), 2, 8, QUAD)]
        + [f32(2, 8, width)]
        + [pltpu.VMEM((4 * size, QUAD), BF16), pltpu.VMEM((QUAD, QUAD), BF16), f32(QUAD, QUAD)]
        + [f32(size, 4 * size)] * 2
        + [sem(2, images), sem(12)]
        + [sem(CHUNKS + 1, red.sems)] * 2
        + [pltpu.SemaphoreType.REGULAR((CHUNKS + 1, red.frees))]
        + [sem(images, 3)] * 4
        + [sem(len(dims) + 1)] * 2
    )
    shape = jax.ShapeDtypeStruct
    square = shape((width, width), F32)
    outs = pl.pallas_call(
        functools.partial(kernel, seq, images, span, red, late, dims),
        out_shape=(
            big(BF16),
            big(BF16),
            f32(CHUNKS, max(CHUNK, red.rows), width),
            f32(VECS, width),
        ),
        in_specs=[hbm, hbm, smem, (vmem,) * len(small)] + [hbm] * 6,
        out_specs=(vmem,) * 4,
        scratch_shapes=scratch,
        compiler_params=pltpu.CompilerParams(
            collective_id=0, has_side_effects=True, vmem_limit_bytes=46 * 2**20
        ),
    )(
        tokens.reshape(flat, width),
        cotangent.reshape(flat, width),
        short_counts,
        small,
        query_weight,
        key_weight,
        value_weight,
        output_weight,
        hidden_weight,
        return_weight,
    )
    rowed = shape((flat, width), BF16)
    smalls = (shape((1,), F32), shape(hidden_bias.shape, F32)) + (shape((width,), F32),) * HB
    bigs = (rowed, rowed, shape(return_weight.shape, F32), shape(hidden_weight.shape, F32)) + (square,) * 4
    outs = pl.pallas_call(
        functools.partial(deliver, 1.0 / (span * seq * (width // HEADS))),
        out_shape=bigs + smalls,
        in_specs=[vmem] * 4,
        out_specs=(hbm,) * 8 + (smem,) + (vmem,) * (1 + HB),
        scratch_shapes=[sem(16)],
        compiler_params=pltpu.CompilerParams(vmem_limit_bytes=4 * 2**20),
    )(*outs)
    ing, lay, gw2, gw1, gwo, gwq, gwk, gwv, peak, hidden = outs[:10]
    n1g, n1b, qb, kb, vb, ob, n2g, n2b, rb = outs[10:]
    lay, ing = lay.reshape(tokens.shape), ing.reshape(tokens.shape)
    attention = (gwq, qb, gwk, kb, gwv, vb, gwo, ob)
    return (lay, ing, peak.reshape(()), n1g, n1b) + attention + (n2g, n2b, gw1, hidden, gw2, rb)


def solution(mesh):
    split = P("dp", "seq", None)
    return jax.shard_map(
        functools.partial(per_device, mesh.shape["seq"], mesh.shape["dp"]),
        mesh=mesh,
        in_specs=(split, P("dp")) + (P(),) * 16 + (split,),
        out_specs=(split, split) + (P(),) * 17,
        check_vma=False,
    )
```

```python
import functools

import jax
import jax.numpy as jnp
from jax import lax
from jax.experimental import pallas as pl
from jax.experimental.pallas import tpu as pltpu
from jax.sharding import PartitionSpec as P

HEADS = 8
LEN_LONG = 3072
LEN_SHORT = 784
EPSILON = 1e-05
F32, BF16 = jnp.float32, jnp.bfloat16
MESH = pl.DeviceIdType.MESH

WIDTH = 512
PART = 512
QUAD = 256
DEPTH = 64
HALVINGS = 3
CHUNK = 1024
CHUNKS = 6
LANDS = 5
SHARES = (4, 3, 1)
LATE_SHARES = (2, 1, 1)
VECS = 16


def mm(a, b):
    return lax.dot_general(a, b, (((1,), (0,)), ((), ())), preferred_element_type=F32)


def nt(a, b):
    return lax.dot_general(a, b, (((1,), (1,)), ((), ())), preferred_element_type=F32)


def tn(a, b):
    return lax.dot_general(a, b, (((0,), (0,)), ((), ())), preferred_element_type=F32)


def colsum(v):
    return jnp.sum(v, axis=0, keepdims=True)


def bit(index, step):
    return lax.rem(lax.div(index, step), 2)


def aligned(v, m=8):
    return v if isinstance(v, int) else pl.multiple_of(v, m)


def coord(dim):
    return bit(lax.axis_index(dim[0]), dim[1])


def peer(dim):
    axis, step = dim
    d, s = lax.axis_index("dp"), lax.axis_index("seq")
    if axis == "dp":
        return (d + step * (1 - 2 * bit(d, step)), s)
    return (d, s + step * (1 - 2 * bit(s, step)))


def remote(src, dst, send, recv, device):
    return pltpu.make_async_remote_copy(
        src_ref=src, dst_ref=dst, send_sem=send, recv_sem=recv, device_id=device, device_id_type=MESH
    )


class Reduce:
    def __init__(self, dims, orders, rows, shares):
        self.core, self.orders = ("dp", 1), orders
        self.half = rows // 2
        unit = self.half // sum(shares)
        self.sizes = [unit * s for s in shares]
        self.starts = [sum(self.sizes[:i]) for i in range(len(shares))]
        self.whole = len(dims) - HALVINGS
        self.between = 2 * HALVINGS + self.whole
        self.steps = self.between + 3
        self.sems = 2 + len(shares) * self.between
        self.dims = [self.core] + dims
        self.frees = len(self.dims) + len(shares) * self.whole
        self.turn = HALVINGS + self.whole + 1
        self.bases = [self.half]
        for p in range(len(shares)):
            self.bases.append(self.bases[-1] + self.offset(p, HALVINGS + self.whole))
        self.rows = self.bases[-1]

    def enter(self):
        self.bits = {dim: coord(dim) for dim in self.dims}
        self.peers = {dim: peer(dim) for dim in self.dims}

    def offset(self, p, k):
        n = self.sizes[p]
        over = max(k - HALVINGS, 0)
        return n - (n >> min(k, HALVINGS)) + over * (n >> HALVINGS)

    def piece(self, p, k):
        at = self.bits[self.core] * self.half + self.starts[p]
        for i in range(k):
            at = at + self.bits[self.orders[p][i]] * (self.sizes[p] >> (i + 1))
        return at

    def copies(self, g, r, ss, rs, stage):
        half = self.half
        if stage in (0, self.steps - 2):
            c = self.bits[self.core]
            mine, other = aligned(c * half), aligned((1 - c) * half)
            if stage == 0:
                dst = r.at[pl.ds(0, half)]
                cp = remote(g.at[pl.ds(other, half)], dst, ss.at[0], rs.at[0], self.peers[self.core])
                return [(cp, mine, 0, half, None, None)]
            part = g.at[pl.ds(mine, half)]
            cp = remote(part, part, ss.at[1], rs.at[1], self.peers[self.core])
            return [(cp, None, None, half, None, None)]
        out = []
        k = stage - 1
        for p, order in enumerate(self.orders):
            n = self.sizes[p]
            sem = 2 + p * self.between + k
            land = self.bases[p] + self.offset(p, k)
            free = None
            if k < HALVINGS:
                m, dim, base = n >> (k + 1), order[k], self.piece(p, k)
                c = self.bits[dim]
                src = g.at[pl.ds(aligned(base + (1 - c) * m), m)]
                dst, to = r.at[pl.ds(land, m)], aligned(base + c * m)
            elif k < HALVINGS + self.whole:
                free = len(self.dims) + p * self.whole + k - HALVINGS
                m, dim, to = n >> HALVINGS, order[k], aligned(self.piece(p, HALVINGS))
                src, dst = g.at[pl.ds(to, m)], r.at[pl.ds(land, m)]
            else:
                i = self.between - 1 - k
                m, dim, to, land = n >> (i + 1), order[i], None, None
                src = dst = g.at[pl.ds(aligned(self.piece(p, i + 1)), m)]
            cp = remote(src, dst, ss.at[sem], rs.at[sem], self.peers[dim])
            out.append((cp, to, land, m, free, self.peers[dim]))
        return out

    def step(self, g, r, ss, rs, fs, k):
        if k > 0:
            for cp, to, land, m, free, device in self.copies(g, r, ss, rs, k - 1):
                cp.wait()
                if to is not None:
                    slab = next(s for s in (64, 48, 32, 24, 16, 8) if m % s == 0)

                    def one(i, c, to=to, land=land, slab=slab):
                        a = pl.ds(pl.multiple_of(to + i * slab, 8), slab)
                        g[a, :] += r[pl.ds(pl.multiple_of(land + i * slab, 8), slab), :]
                        return c

                    lax.fori_loop(0, m // slab, one, 0)
                    if free is not None:
                        pl.semaphore_signal(fs.at[free], inc=1, device_id=device, device_id_type=MESH)
        if k == HALVINGS + 1:
            for i, dim in enumerate(self.dims):
                pl.semaphore_signal(fs.at[i], inc=1, device_id=self.peers[dim], device_id_type=MESH)
        if k == self.turn:
            for i in range(len(self.dims)):
                pl.semaphore_wait(fs.at[i], 1)
        if k == self.turn + 1:
            for i in range(len(self.dims), self.frees):
                pl.semaphore_wait(fs.at[i], 1)
        if k < self.steps - 1:
            for cp, *_ in self.copies(g, r, ss, rs, k):
                cp.start()


class Scan:
    def __init__(self, seq, back, own, rx1, rxp, txp, tx2, rx2, prior, ss, rs):
        self.hops = seq // 2
        place = lax.axis_index("seq")
        self.dp, self.place = lax.axis_index("dp"), place
        lo, hi = lax.rem(place, 2), lax.div(place, 2)
        self.partner = (self.dp, place + 1 - 2 * lo)
        self.next = (self.dp, place - 2 if back else place + 2)
        self.lo = 1 - lo if back else lo
        self.hi = self.hops - 1 - hi if back else hi
        self.own, self.rx1, self.rxp, self.txp = own, rx1, rxp, txp
        self.tx2, self.rx2, self.prior, self.ss, self.rs = tx2, rx2, prior, ss, rs

    def first(self, i):
        src = self.own.at[i, 1 - self.lo]
        return remote(src, self.rx1.at[i], self.ss.at[i, 0], self.rs.at[i, 0], self.partner)

    def chain(self, i):
        return remote(
            self.txp.at[i], self.rxp.at[i], self.ss.at[i, 1], self.rs.at[i, 1], self.next
        )

    def last(self, i):
        return remote(
            self.tx2.at[i], self.rx2.at[i], self.ss.at[i, 2], self.rs.at[i, 2], self.partner
        )

    def begin(self, i):
        self.first(i).start()

    def hop(self, i):
        @pl.when(self.hi == 0)
        def _():
            self.rxp[i] = jnp.zeros_like(self.rxp[i])

        self.first(i).wait()
        mine = self.own[i, self.lo]
        other = self.rx1[i]

        @pl.when(self.hi > 0)
        def _():
            self.chain(i).wait_recv()

        came = self.rxp[i]

        @pl.when(self.hi < self.hops - 1)
        def _():
            self.txp[i] = came + mine + other
            self.chain(i).start()

        upper = self.lo.astype(F32)
        self.tx2[i] = came + (1.0 - upper) * mine
        self.last(i).start()
        self.prior[i, self.lo] = came + upper * other

    def end(self, i):
        self.last(i).wait()

        @pl.when(self.hi < self.hops - 1)
        def _():
            self.chain(i).wait_send()

        self.prior[i, 1 - self.lo] = self.rx2[i]


def norm_parts(v):
    centre = v - jnp.mean(v, axis=-1, keepdims=True)
    rate = lax.rsqrt(jnp.mean(centre * centre, axis=-1, keepdims=True) + EPSILON)
    return centre * rate, rate


def norm_back(grad, unit, rate, gain):
    inner = grad * gain
    shift = jnp.mean(inner, axis=-1, keepdims=True)
    scale = jnp.mean(inner * unit, axis=-1, keepdims=True)
    return rate * (inner - shift - unit * scale)


def feature(v):
    return jnp.where(v > 0, v + 1.0, jnp.exp(jnp.minimum(v, 0.0)))


def normal_parts(u):
    e = jnp.exp(-0.5 * u * u)
    t = 1.0 / (1.0 + 0.3275911 * 0.7071067811865476 * jnp.abs(u))
    poly = 0.7107068705 + t * (-0.7265760135 + t * 0.5307027145)
    tail = t * (0.127414796 + t * (-0.142248368 + t * poly)) * e
    return jnp.where(u > 0, 1.0 - tail, tail), e * 0.3989422804014327


def split(v):
    high = v.astype(BF16)
    return high, (v - high.astype(F32)).astype(BF16)


def four(v):
    return jnp.concatenate([v] * 4, axis=0)


def fold(v):
    return v[0:64] + v[64:128] + v[128:192] + v[192:256]


def spread(v):
    inside = lax.broadcasted_iota(jnp.int32, (v.shape[0], 128), 1) < DEPTH
    out = []
    for t in range(2):
        tile = v[:, t * 128 : (t + 1) * 128]
        turned = pltpu.roll(tile, DEPTH, 1)
        out += [jnp.where(inside, tile, turned), jnp.where(inside, turned, tile)]
    return out


N1G, N1B, QB, KB, VB, OB, N2G, N2B, RB, HB = range(10)
PEAK = 13


def kernel(
    seq,
    images,
    span,
    red,
    late,
    dims,
    tok_hbm,
    cot_hbm,
    short_ref,
    vec_refs,
    wq_hbm,
    wk_hbm,
    wv_hbm,
    wo_hbm,
    w1_hbm,
    w2_hbm,
    x,
    ct,
    g,
    sums_ref,
    fq,
    fk,
    vb,
    at,
    iv,
    si,
    out,
    d2,
    ws,
    w1,
    w2,
    lands,
    vec,
    sb,
    srx,
    own,
    rx1,
    f_rxp,
    b_rxp,
    txp,
    tx2,
    rx2,
    f_prior,
    b_prior,
    mu,
    dgt,
    gsum,
    late_sums,
    mx,
    bo,
    bof,
    cm,
    cmt,
    in_sem,
    w_sem,
    red_ss,
    red_rs,
    red_fs,
    f_ss,
    f_rs,
    b_ss,
    b_rs,
    s_ss,
    s_rs,
):
    per = 2 if images % 2 == 0 else 1
    blocks = images // per
    rows = per * span
    size = 128 if span % 128 == 0 else span
    parts = span // size
    place = lax.axis_index("seq")
    small = [("dp", 1)] + dims
    red.enter()
    late.enter()

    step_s = images
    step_b = step_s + images
    step_f = step_b + 2 * blocks
    step_g = step_f + 2 * blocks
    step_q = step_g + 2 * blocks
    step_k = step_q + images
    step_n = step_k + 2 * images
    step_d = step_n + blocks
    spans = [13] * step_b + [35, 34] * blocks + [34] * (2 * blocks) + [34, 44] * blocks
    spans += [23] * images + [16] * (2 * images) + [11] * blocks
    clock = [sum(spans[: u + 1]) for u in range(len(spans))]
    clock += [clock[-1] + 20 * n for n in range(1, 80)]

    def places(start, offsets):
        return [next(u for u, t in enumerate(clock) if t >= clock[start] + d) for d in offsets]

    slow, fast = red_offsets(red, RED_GAPS), red_offsets(late, LATE_GAPS)
    when = [places(start, slow) for start in (step_f - 1, step_f + blocks - 1, step_g - 1, step_q - 2)]
    when.append(places(max(step_k - 1, when[1][red.turn + 1]), red_offsets(red, MID_GAPS)))
    when.append(places(max(step_k + images - 1, when[2][red.turn + 1]), fast))
    when.append(places(max(step_n - 1, when[2][red.turn + 1]), fast))
    total_steps = max([step_d + len(small)] + [places_of[-1] for places_of in when]) + 1

    def image(i):
        return pl.ds(pl.multiple_of(i * span, 16), span)

    def block(b):
        return pl.ds(pl.multiple_of(b * rows, 16), rows)

    def spot(i, c):
        return pl.ds(pl.multiple_of(i * span + c * size, 16), size)

    def fetch(hbm, ref, sem, i):
        return pltpu.make_async_copy(hbm.at[image(i)], ref.at[image(i)], sem.at[i])

    fetch(tok_hbm, x, in_sem.at[0], 0).start()
    loads = [
        pltpu.make_async_copy(h, ws.at[i], w_sem.at[i])
        for i, h in enumerate((wq_hbm, wk_hbm, wv_hbm, wo_hbm))
    ]
    for load in loads[:3]:
        load.start()
    for i in range(1, images):
        fetch(tok_hbm, x, in_sem.at[0], i).start()
    loads[3].start()

    def weights(j):
        cols = pl.ds(j * PART, PART)
        return (
            pltpu.make_async_copy(w1_hbm.at[:, cols], w1.at[j % 2], w_sem.at[4 + j]),
            pltpu.make_async_copy(w2_hbm.at[cols, :], w2.at[j % 2], w_sem.at[8 + j]),
        )

    def fill(j):
        for load in weights(j):
            load.start()

    def filled(j):
        for load in weights(j):
            load.wait()

    fill(0)
    fill(1)
    for i in range(images):
        fetch(cot_hbm, ct, in_sem.at[1], i).start()

    barrier = pltpu.get_barrier_semaphore()
    chain = [(lax.axis_index("dp"), lax.rem(place + d, seq)) for d in (2, seq - 2)]
    friends = [peer(d) for d in small] + chain
    for friend in friends:
        pl.semaphore_signal(barrier, inc=1, device_id=friend, device_id_type=MESH)

    for i, ref in enumerate(vec_refs):
        vec[i : i + ref.shape[0] // WIDTH, :] = ref[...].astype(F32).reshape(-1, WIDTH)

    def iota(shape, axis):
        return lax.broadcasted_iota(jnp.int32, shape, axis)

    tile = (QUAD, QUAD)
    bof[...] = jnp.where(iota(tile, 0) // DEPTH == iota(tile, 1) // DEPTH, 1.0, 0.0)
    bo[...] = bof[...].astype(BF16)
    tall = (4 * size, QUAD)
    mx[...] = jnp.where(iota(tall, 0) // size == iota(tall, 1) // DEPTH, 1.0, 0.0).astype(BF16)
    wide = (size, 4 * size)
    cm[...] = jnp.where(iota(wide, 1) % size <= iota(wide, 0), 1.0, 0.0)
    cmt[...] = jnp.where(iota(wide, 1) % size >= iota(wide, 0), 1.0, 0.0)
    sb[...] = jnp.zeros_like(sb)
    late_sums[...] = jnp.zeros_like(late_sums)

    def clear(c, ignored):
        def inner(k, ignored):
            g[c, pl.ds(pl.multiple_of(k * 64, 8), 64), :] = jnp.zeros((64, WIDTH), F32)
            return ignored

        return lax.fori_loop(0, CHUNK // 64, inner, ignored)

    def row(i):
        return vec[i : i + 1, :]

    def add(i, v):
        sb[i : i + 1, :] += v

    def limit(i):
        return jnp.where(i < short_ref[0], LEN_SHORT, LEN_LONG)

    def positions(start, count, width):
        return iota((count, width), 0) + (place * span + start)

    forward = Scan(seq, False, own, rx1, f_rxp, txp, tx2, rx2, f_prior, f_ss, f_rs)
    backward = Scan(seq, True, own, rx1, b_rxp, txp, tx2, rx2, b_prior, b_ss, b_rs)
    halves = [slice(q * QUAD, (q + 1) * QUAD) for q in range(2)]
    cells = [(q, c) for q in range(2) for c in range(parts)]

    def read(ref, i, q, c):
        return ref[spot(i, c), halves[q]]

    def together(pieces):
        rows_of = [jnp.concatenate(pieces[q * parts : (q + 1) * parts], axis=0) for q in range(2)]
        return jnp.concatenate(rows_of, axis=1)

    def put(i, q, state, total):
        own[i, q, 0:64, :] = fold(state)
        own[i, q, 64:65, :] = total

    def known(ref, i, q):
        return four(ref[i, q, 0:64, :]) * bof[...], ref[i, q, 64:65, :]

    def centre(i, q):
        return mu[pl.ds(i, 1), halves[q]]

    def head_sums(v):
        high, low = split(v)
        return mm(high, bo[...]) + mm(low, bo[...])

    def project(i):
        fetch(tok_hbm, x, in_sem.at[0], i).wait()

        @pl.when(i == 0)
        def _():
            for load in loads[:3]:
                load.wait()

        part = image(i)
        unit, _ = norm_parts(x[part, :].astype(F32))
        first = (unit * row(N1G) + row(N1B)).astype(BF16)
        key = feature(mm(first, ws[1]) + row(KB))
        inside = positions(0, span, WIDTH) < limit(i)
        key = jnp.where(inside, key, 0.0).astype(BF16)
        fk[part, :] = key
        value = (mm(first, ws[2]) + row(VB)).astype(BF16)
        vb[part, :] = value
        total = colsum(key.astype(F32))
        for q, cols in enumerate(halves):
            put(i, q, tn(key[:, cols], value[:, cols]) * bof[...], total[:, cols])
        fq[part, :] = feature(mm(first, ws[0]) + row(QB)).astype(BF16)

        @pl.when(i == 0)
        def _():
            pl.semaphore_wait(barrier, len(friends))

        forward.begin(i)

    def within(i):
        query = [read(fq, i, *o) for o in cells]
        score = [(nt(u, four(read(fk, i, *o)) * mx[...]) * cm[...]).astype(BF16) for u, o in zip(query, cells)]
        num = [mm(v, four(read(vb, i, *o)) * mx[...]) for v, o in zip(score, cells)]
        den = [mm(v, mx[...]) for v in score]
        for n, d, (q, c) in zip(num, den, cells):
            out[spot(i, c), halves[q]] = n
            d2[spot(i, c), halves[q]] = d

        @pl.when(i < LANDS)
        def _():
            clear(i, 0)

    def entering(i, q):
        state, total = known(f_prior, i, q)
        states, totals = [], []
        for c in range(parts):
            states.append(split(state))
            totals.append(total)
            if c < parts - 1:
                key = read(fk, i, q, c)
                state = state + tn(key, read(vb, i, q, c)) * bof[...]
                total = total + colsum(key.astype(F32))
        return states, totals

    def attend(i):
        forward.end(i)
        for q, cols in enumerate(halves):
            state, total = f_prior[i, q, 0:64, :], f_prior[i, q, 64:65, :]
            count = total + own[i, q, 64:65, :]
            count = head_sums(jnp.broadcast_to(count, (8, QUAD)))[0:1]
            off = colsum(state + own[i, q, 0:64, :]) / count
            mu[pl.ds(i, 1), cols] = off
        ahead = [entering(i, q) for q in range(2)]
        inside = positions(0, span, QUAD) < limit(i)
        for q, c in cells:
            at_spot = (spot(i, c), halves[q])
            query, off = fq[at_spot], centre(i, q)
            high, low = ahead[q][0][c]
            n = out[at_spot] + mm(query, high) + mm(query, low)
            d = d2[at_spot] + head_sums(query.astype(F32) * ahead[q][1][c])
            inverse = 1.0 / d
            at[at_spot] = (n * inverse - off).astype(BF16)
            iv[at_spot] = inverse.astype(BF16)
            peak = jnp.max(jnp.where(inside[c * size : (c + 1) * size], d, 0.0), axis=0, keepdims=True)
            sb[PEAK : PEAK + 1, halves[q]] = jnp.maximum(sb[PEAK : PEAK + 1, halves[q]], peak)
        part = image(i)
        mid = x[part, :].astype(F32) + mm(attended(i), ws[3]) + row(OB)
        unit, _ = norm_parts(mid)
        si[part, :] = (unit * row(N2G) + row(N2B)).astype(BF16)
        out[part, :] = mid + row(RB)
        d2[part, :] = jnp.zeros((span, WIDTH), F32)
        fetch(cot_hbm, ct, in_sem.at[1], i).wait()
        add(RB, colsum(ct[part, :].astype(F32)))

    def attended(i):
        return (at[image(i), :].astype(F32) + mu[pl.ds(i, 1), :]).astype(BF16)

    def feed(j, b):
        normed, grad = si[block(b), :], ct[block(b), :]
        up, down = w1[lax.rem(j, 2)], w2[lax.rem(j, 2)]
        act, pre = [], []
        for im in range(per):
            part = slice(im * span, (im + 1) * span)
            hidden = mm(normed[part], up) + vec[pl.ds(HB + j, 1), :]
            back = nt(grad[part], down)
            cdf, pdf = normal_parts(hidden)
            act.append((hidden * cdf).astype(BF16))
            pre.append((back * (cdf + hidden * pdf)).astype(BF16))
            out[image(b * per + im), :] += mm(act[im], down)
            d2[image(b * per + im), :] += nt(pre[im], up)
        act, pre = jnp.concatenate(act, axis=0), jnp.concatenate(pre, axis=0)
        g[j, 0:512, :] += tn(act, grad)
        g[j, 512:1024, :] += tn(normed, pre)
        sb[pl.ds(HB + j, 1), :] += colsum(pre.astype(F32))

    def norm_two(i):
        part = image(i)
        attn = attended(i)
        unit, rate = norm_parts(x[part, :].astype(F32) + mm(attn, ws[3]) + row(OB))
        grad = d2[part, :]
        add(N2G, colsum(grad * unit))
        add(N2B, colsum(grad))
        residual = ct[part, :].astype(F32) + norm_back(grad, unit, rate, row(N2G))
        d2[part, :] = residual
        ct[part, :] = out[part, :].astype(BF16)
        low = residual.astype(BF16)
        mixed_grad = nt(low, ws[3])
        inverse = iv[part, :].astype(F32)
        num_grad = (mixed_grad * inverse).astype(BF16)
        si[part, :] = num_grad
        inner = num_grad.astype(F32) * (at[part, :].astype(F32) + mu[pl.ds(i, 1), :])
        den_grad = jnp.concatenate([-head_sums(inner[:, cols]) for cols in halves], axis=1)
        high, low_part = split(den_grad)
        iv[part, :] = high
        at[part, :] = low_part
        query = fq[part, :]
        totals = den_grad * query.astype(F32)
        totals = [colsum(totals[c * size : (c + 1) * size]) for c in range(parts)]
        for c in range(1, parts):
            for q, cols in enumerate(halves):
                gsum[i * parts + c, q, 0:1, :] = totals[c][:, cols]
        total = functools.reduce(lambda a, b: a + b, totals)
        for q, cols in enumerate(halves):
            put(i, q, tn(query[:, cols], num_grad[:, cols]) * bof[...], total[:, cols])
        backward.begin(i)
        pick = jnp.where(iota((8, WIDTH), 1) == iota((8, WIDTH), 0) * DEPTH, 1.0, 0.0).astype(BF16)
        line = nt(pick, high) + nt(pick, low_part)
        dgt[i, 0, 0:4, :] = line[0:4]
        dgt[i, 1, 0:4, :] = line[4:8]
        g[4, 0:512, :] += tn(attn, low)
        add(OB, colsum(low.astype(F32)))

    def query_side(i):
        unit, _ = norm_parts(x[image(i), :].astype(F32))
        first = (unit * row(N1G) + row(N1B)).astype(BF16)
        ahead = [entering(i, q) for q in range(2)]
        num_grad = [read(si, i, *o) for o in cells]
        den_grad = [read(iv, i, *o).astype(F32) + read(at, i, *o).astype(F32) for o in cells]
        at[image(i), :] = first
        back = [nt(n, four(read(vb, i, *o)) * mx[...]) for n, o in zip(num_grad, cells)]
        back = [
            ((v + jnp.concatenate(spread_rows(d), axis=1)) * cm[...]).astype(BF16)
            for v, d in zip(back, den_grad)
        ]
        side = [mm(v, four(read(fk, i, *o)) * mx[...]) for v, o in zip(back, cells)]
        low = []
        for u, n, d, (q, c) in zip(side, num_grad, den_grad, cells):
            high, part = ahead[q][0][c]
            grad = u + nt(n, high) + nt(n, part) + d * ahead[q][1][c]
            low.append((grad * jnp.minimum(read(fq, i, q, c).astype(F32), 1.0)).astype(BF16))
        low = together(low)
        g[4, 512:1024, :] += tn(first, low)
        add(QB, colsum(low.astype(F32)))
        out[image(i), :] = nt(low, ws[0])

    def spread_rows(v):
        return [u[:, :size] for u in spread(v)]

    def key_side(i, q):
        cols = pl.ds(pl.multiple_of(q * QUAD, QUAD), QUAD)
        first = at[image(i), :]
        state, total = known(b_prior, i, q)
        states, totals = [], []
        for c in reversed(range(parts)):
            states.insert(0, split(state))
            totals.insert(0, total)
            if c > 0:
                state = state + tn(fq[spot(i, c), cols], si[spot(i, c), cols]) * bof[...]
                total = total + gsum[i * parts + c, q, 0:1, :]
        wide_query = [four(fq[spot(i, c), cols]) * mx[...] for c in range(parts)]
        wide_num = [four(si[spot(i, c), cols]) * mx[...] for c in range(parts)]
        key = [fk[spot(i, c), cols] for c in range(parts)]
        value = [vb[spot(i, c), cols] for c in range(parts)]
        score = [(nt(k, u) * cmt[...]).astype(BF16) for k, u in zip(key, wide_query)]
        value_part = [mm(v, u) for v, u in zip(score, wide_num)]
        back = []
        for c in range(parts):
            line = [dgt[i, q, h : h + 1, c * size : (c + 1) * size] for h in range(4)]
            line = jnp.concatenate(line, axis=1)
            back.append(((nt(value[c], wide_num[c]) + line) * cmt[...]).astype(BF16))
        key_part = [mm(v, u) for v, u in zip(back, wide_query)]
        low_k, low_v = [], []
        for c in range(parts):
            (high, part), total = states[c], totals[c]
            grad = key_part[c] + nt(value[c], high) + nt(value[c], part) + total
            low_k.append((grad * jnp.minimum(key[c].astype(F32), 1.0)).astype(BF16))
            low_v.append((value_part[c] + mm(key[c], high)).astype(BF16))
        low_k, low_v = jnp.concatenate(low_k, axis=0), jnp.concatenate(low_v, axis=0)
        both = jnp.concatenate([low_k, low_v], axis=1)
        g[5, pl.ds(pl.multiple_of(q * 512, 512), 512), :] += tn(first, both)
        late_sums[q, 0:1, :] += colsum(both.astype(F32))
        out[image(i), :] += nt(low_k, ws[1, :, cols]) + nt(low_v, ws[2, :, cols])

    def norm_one(i):
        part = image(i)
        unit, rate = norm_parts(x[part, :].astype(F32))
        grad = out[part, :]
        add(N1G, colsum(grad * unit))
        add(N1B, colsum(grad))
        x[part, :] = (d2[part, :] + norm_back(grad, unit, rate, row(N1G))).astype(BF16)

    def over(body):
        def run(b):
            def one(im, ignored):
                body(b * per + im)
                return ignored

            lax.fori_loop(0, per, one, 0)

        return run

    events = [(u, c, k) for c, line in enumerate(when) for k, u in enumerate(line)]
    events.sort(key=lambda e: (e[0], e[1] if e[0] < step_n else -e[1]))

    def advance(c, k):
        sems = (red_ss.at[c], red_rs.at[c], red_fs.at[c])
        if c < 5:
            land = g.at[CHUNKS - 1] if c == 0 else lands.at[c - 1 if c < 4 else 0]
            red.step(g.at[c], land, *sems, k)
        else:
            mine = g.at[5, pl.ds((c - 5) * 512, 512)]
            late.step(mine, lands.at[1, pl.ds((c - 5) * late.rows, late.rows)], *sems, k)

    def due(u, start, stop):
        for at_step, c, k in events:
            if isinstance(u, int):
                if at_step == u:
                    advance(c, k)
            elif start <= at_step < stop:

                @pl.when(u == at_step)
                def _(c=c, k=k):
                    advance(c, k)

    def swap(k):
        return remote(sb, srx.at[k], s_ss.at[k], s_rs.at[k], peer(small[k]))

    def swaps(u):
        peaks = iota((VECS, WIDTH), 0) == PEAK
        for k in range(len(small) + 1):

            if u == step_d + k:
                if k > 0:
                    swap(k - 1).wait()
                    came = srx[k - 1]
                    sb[...] = jnp.where(peaks, jnp.maximum(sb[...], came), sb[...] + came)
                if k < len(small):
                    swap(k).start()

    def hops(scan, start, stop):
        def one(i, ignored):
            scan.hop(i)
            return ignored

        lax.fori_loop(start, stop, one, 0)

    def ready(scan, begun, now, least):
        count = jnp.maximum(0, least)
        for i in range(images):
            arrived = begun[i] + 42 + 39 * scan.hi <= now
            count = jnp.maximum(count, jnp.where(arrived, i + 1, 0))
        return count

    opened = [13 * (i + 1) + 3 * i for i in range(images)]
    turned = [56 + 78 * (i // per) + 22 * (i % per) for i in range(images)]

    def forward_by(u):
        v = u - step_b
        late = 13 * step_b + 39 * v
        now = jnp.where(u < step_b, 13 * (u + 1), late)
        least = jnp.where(u < step_b, 0, per * (1 + lax.div(v, 2)))
        return ready(forward, opened, now, jnp.clip(least, 0, images))

    def hops_forward(u):
        hops(forward, jnp.where(u == 0, 0, forward_by(u - 1)), forward_by(u))

    def backward_by(u):
        v, w, y = u - step_g, u - step_q, u - step_k
        in_g = 78 * lax.div(v, 2) + jnp.where(lax.rem(v, 2) == 0, 34, 78)
        now = jnp.where(u < step_q, in_g, jnp.where(u < step_k, 78 * blocks + 24 * (w + 1), 78 * blocks + 24 * images + 17 * (y + 1)))
        least = jnp.clip(jnp.where(u < step_k - 1, 0, y + 2), 0, images)
        return ready(backward, turned, now - 20, least)

    def hops_backward(u):
        hops(backward, jnp.where(u == step_g, 0, backward_by(u - 1)), backward_by(u))

    def run(start, stop, body):
        def one(u, ignored):
            body(u)
            return ignored

        lax.fori_loop(start, stop, one, 0)

    def opening(u):
        @pl.when(u < step_s)
        def _():
            project(u)

        @pl.when(u >= step_s)
        def _():
            within(u - step_s)

        hops_forward(u)

    def part_first(u):
        b = lax.div(u - step_b, 2)
        hops_forward(u)

        @pl.when(lax.rem(u - step_b, 2) == 0)
        def _():
            over(attend)(b)

        @pl.when(lax.rem(u - step_b, 2) == 1)
        def _():
            feed(0, b)

    def part_between(u):
        @pl.when(u == step_f + blocks)
        def _():
            fill(3)
            filled(2)

        feed(1 + lax.div(u - step_f, blocks), lax.rem(u - step_f, blocks))
        due(u, step_f, step_g)

    def part_last(u):
        b = lax.div(u - step_g, 2)

        @pl.when(lax.rem(u - step_g, 2) == 0)
        def _():
            feed(3, b)

        @pl.when(lax.rem(u - step_g, 2) == 1)
        def _():
            over(norm_two)(b)

        due(u, step_g, step_q)
        hops_backward(u)

    def part_query(u):
        query_side(u - step_q)
        due(u, step_q, step_k)
        hops_backward(u)

    def part_key(u):
        i, q = lax.rem(u - step_k, images), lax.div(u - step_k, images)

        @pl.when(q == 0)
        def _():
            backward.end(i)

        key_side(i, q)
        due(u, step_k, step_n)
        hops_backward(u)

    def closing(u):
        if u < step_d:
            b = u - step_n
            over(norm_one)(b)
        due(u, u, u + 1)
        swaps(u)

    run(0, step_b, opening)
    loads[3].wait()
    filled(0)
    run(step_b, step_f, part_first)
    due(step_f - 1, 0, 0)
    fill(2)
    filled(1)
    run(step_f, step_g, part_between)
    filled(3)
    run(step_g, step_q, part_last)
    run(step_q, step_k, part_query)
    clear(CHUNKS - 1, 0)
    run(step_k, step_n, part_key)
    for q, cols in enumerate(halves):
        sb[KB : KB + 1, cols] = late_sums[q, 0:1, 0:QUAD]
        sb[VB : VB + 1, cols] = late_sums[q, 0:1, QUAD:WIDTH]
    for u in range(step_n, total_steps):
        closing(u)
    sums_ref[...] = sb[...]


def deliver(scale, ing, lay, g, sums, *refs):
    ing_out, lay_out, gw2, gw1, gwo, gwq, gwk, gwv, peak, hidden = refs[:10]
    sems = refs[-1]
    pairs = [(ing, ing_out), (lay, lay_out)]
    for c in range(4):
        cols = pl.ds(c * PART, PART)
        pairs += [(g.at[c, pl.ds(0, 512)], gw2.at[cols, :]), (g.at[c, pl.ds(512, 512)], gw1.at[:, cols])]
    pairs += [(g.at[4, pl.ds(0, 512)], gwo), (g.at[4, pl.ds(512, 512)], gwq)]
    for q in range(2):
        rows, cols = pl.ds(q * 512, 512), pl.ds(q * QUAD, QUAD)
        pairs += [
            (g.at[5, rows, pl.ds(0, QUAD)], gwk.at[:, cols]),
            (g.at[5, rows, pl.ds(QUAD, QUAD)], gwv.at[:, cols]),
        ]
    copies = [pltpu.make_async_copy(a, b, sems.at[i]) for i, (a, b) in enumerate(pairs)]
    for copy in copies:
        copy.start()
    peak[0] = jnp.max(sums[PEAK : PEAK + 1, :]) * scale
    hidden[...] = sums[HB : HB + 4, :].reshape(4 * WIDTH)
    for i, ref in enumerate(refs[10:-1]):
        ref[...] = sums[i : i + 1, :].reshape(WIDTH)
    for copy in copies:
        copy.wait()


RED_GAPS = (52, 130, 104, 78, 65, 65, 91, 130, 65)
MID_GAPS = (35, 80, 55, 45, 40, 40, 50, 80, 40)
LATE_GAPS = (30, 55, 40, 32, 32, 32, 40, 55, 30)


def red_offsets(red, gaps):
    gaps = gaps[:4] + gaps[4:5] * (red.steps - 9) + gaps[5:] if red.steps > 9 else gaps[: red.steps - 1]
    return [sum(gaps[:k]) for k in range(red.steps)]


def per_device(
    seq,
    dp,
    tokens,
    short_counts,
    norm1_gain,
    norm1_bias,
    query_weight,
    query_bias,
    key_weight,
    key_bias,
    value_weight,
    value_bias,
    output_weight,
    output_bias,
    norm2_gain,
    norm2_bias,
    hidden_weight,
    hidden_bias,
    return_weight,
    return_bias,
    cotangent,
):
    images, span, width = tokens.shape
    flat = images * span
    per = 2 if images % 2 == 0 else 1
    blocks = images // per
    size = 128 if span % 128 == 0 else span
    dims = [("dp", 1 << k) for k in range(1, dp.bit_length() - 1)]
    dims = dims + [("seq", 1 << k) for k in range(seq.bit_length() - 1)]
    turn = (len(dims) - 1) // 3
    orders = [dims[i * turn :] + dims[: i * turn] for i in range(3)]
    red = Reduce(dims, orders, CHUNK, SHARES)
    late = Reduce(dims, orders, CHUNK // 2, LATE_SHARES)
    small = (norm1_gain, norm1_bias, query_bias, key_bias, value_bias, output_bias, norm2_gain, norm2_bias, return_bias)
    small = small + (hidden_bias,)
    hbm = pl.BlockSpec(memory_space=pl.ANY)
    vmem = pl.BlockSpec(memory_space=pltpu.VMEM)
    smem = pl.BlockSpec(memory_space=pltpu.SMEM)
    state = (images, 72, QUAD)
    pair = (images, 2, 72, QUAD)
    big = lambda kind: pltpu.VMEM((flat, width), kind)
    f32 = lambda *shape: pltpu.VMEM(shape, F32)
    sem = lambda *shape: pltpu.SemaphoreType.DMA(shape)
    scratch = (
        [big(BF16)] * 6
        + [big(F32)] * 2
        + [pltpu.VMEM((4, width, width), BF16)]
        + [pltpu.VMEM((2, width, PART), BF16), pltpu.VMEM((2, PART, width), BF16)]
        + [f32(3, max(CHUNK, red.rows, 2 * late.rows), width)]
        + [f32(VECS, width)] * 2
        + [f32(len(dims) + 1, VECS, width)]
        + [f32(*pair)]
        + [f32(*state)] * 6
        + [f32(*pair)] * 2
        + [f32(-(-images // 8) * 8, width), f32(images, 2, 8, span), f32(images * (span // size), 2, 8, QUAD)]
        + [f32(2, 8, width)]
        + [pltpu.VMEM((4 * size, QUAD), BF16), pltpu.VMEM((QUAD, QUAD), BF16), f32(QUAD, QUAD)]
        + [f32(size, 4 * size)] * 2
        + [sem(2, images), sem(12)]
        + [sem(CHUNKS + 1, red.sems)] * 2
        + [pltpu.SemaphoreType.REGULAR((CHUNKS + 1, red.frees))]
        + [sem(images, 3)] * 4
        + [sem(len(dims) + 1)] * 2
    )
    shape = jax.ShapeDtypeStruct
    square = shape((width, width), F32)
    outs = pl.pallas_call(
        functools.partial(kernel, seq, images, span, red, late, dims),
        out_shape=(
            big(BF16),
            big(BF16),
            f32(CHUNKS, max(CHUNK, red.rows), width),
            f32(VECS, width),
        ),
        in_specs=[hbm, hbm, smem, (vmem,) * len(small)] + [hbm] * 6,
        out_specs=(vmem,) * 4,
        scratch_shapes=scratch,
        compiler_params=pltpu.CompilerParams(
            collective_id=0, has_side_effects=True, vmem_limit_bytes=46 * 2**20
        ),
    )(
        tokens.reshape(flat, width),
        cotangent.reshape(flat, width),
        short_counts,
        small,
        query_weight,
        key_weight,
        value_weight,
        output_weight,
        hidden_weight,
        return_weight,
    )
    rowed = shape((flat, width), BF16)
    smalls = (shape((1,), F32), shape(hidden_bias.shape, F32)) + (shape((width,), F32),) * HB
    bigs = (rowed, rowed, shape(return_weight.shape, F32), shape(hidden_weight.shape, F32)) + (square,) * 4
    outs = pl.pallas_call(
        functools.partial(deliver, 1.0 / (span * seq * (width // HEADS))),
        out_shape=bigs + smalls,
        in_specs=[vmem] * 4,
        out_specs=(hbm,) * 8 + (smem,) + (vmem,) * (1 + HB),
        scratch_shapes=[sem(16)],
        compiler_params=pltpu.CompilerParams(vmem_limit_bytes=4 * 2**20),
    )(*outs)
    ing, lay, gw2, gw1, gwo, gwq, gwk, gwv, peak, hidden = outs[:10]
    n1g, n1b, qb, kb, vb, ob, n2g, n2b, rb = outs[10:]
    lay, ing = lay.reshape(tokens.shape), ing.reshape(tokens.shape)
    attention = (gwq, qb, gwk, kb, gwv, vb, gwo, ob)
    return (lay, ing, peak.reshape(()), n1g, n1b) + attention + (n2g, n2b, gw1, hidden, gw2, rb)


def solution(mesh):
    split = P("dp", "seq", None)
    return jax.shard_map(
        functools.partial(per_device, mesh.shape["seq"], mesh.shape["dp"]),
        mesh=mesh,
        in_specs=(split, P("dp")) + (P(),) * 16 + (split,),
        out_specs=(split, split) + (P(),) * 17,
        check_vma=False,
    )
```
